32 devices in a mesh: seg: 8 (over z, y), grp: 4 (over x, core).
Axes of the slice: x: 2, y: 2, z: 4, core: 2. Of those that a mesh axis runs over, the one named last changes fastest.
Arguments:
- spectra: bfloat16 [8, 2, 128, 12288], P(None, None, None, ('seg', 'grp'))
- band_bins: int32 [2, 2], replicated, may hold values from 0 to 80, as said below
- far_list: int32 [4, 8, 8, 4, 3], P('grp'), may hold values from 0 to 2, as said below
- far_count: int32 [4, 8, 8], P('grp'), may hold values from 0 to 4, as said below
Outputs:
- near_corr: bfloat16 [2, 2, 12288, 1536], P(None, None, ('seg', 'grp'))
- far_corr: bfloat16 [8, 4, 8, 4, 2, 128, 128], P('seg', 'grp')
The draws below stay inside these ranges and needn't reach their ends.
Inputs may be any that keep to these rules, and one draw needn't show every extreme that they name: band_bins[b, 0] + 48 <= 128 and 1 <= band_bins[b, 1] <= 48; band 0 has exactly 48 bins; one band starts at bin 0 and the other at bin 128 - 48. far_list entries: row and column blocks 0 to 2, band 0 or 1. far_count is 0 where owner and source group are the same; every owner has some source group with exactly 4.
All inputs are finite; a program needn't handle non-finite values.
Results may differ from the reference program's by a relative error of at most 0.0058.
Values may be sent and summed in bfloat16 or wider, within the bound.
A program may use at most 192 MiB of HBM per device.

```python
import math
import jax
import jax.numpy as jnp
from jax import lax

W = 8
F = 128
BAND_MAX = 48
SMOOTH = 4
BLOCK = 128
BLK_DEV = 3
CAP = 4
SEGS = 8
GRPS = 4
NBLK = 96
NCH = 12288
GCH = 1536
DEVICES = 32


def draw_spectra(key, part):
    key_amp = jax.random.fold_in(key, 11)
    key_gain = jax.random.fold_in(key, 12)
    key_noise = jax.random.fold_in(key, 13)
    amplitude = jnp.exp(jax.random.uniform(key_amp, (F, NCH), jnp.float32, math.log(0.1), math.log(10.0)))
    gains = jax.random.uniform(key_gain, (W, NCH), jnp.float32, 0.5, 2.0)
    noise = jax.random.normal(key_noise, (W, 2, F, NCH), jnp.float32)
    values = noise * amplitude[None, None] * gains[:, None, None, :]
    return values.astype(jnp.bfloat16)


def draw_band_bins(key, part):
    key_start = jax.random.fold_in(key, 21)
    key_count = jax.random.fold_in(key, 22)
    flip = jax.random.randint(key_start, (1,), 0, 2, jnp.int32)
    first = flip * (F - BAND_MAX)
    other = (1 - flip) * (F - BAND_MAX)
    starts = jnp.concatenate([first, other])
    second = jax.random.randint(key_count, (1,), BAND_MAX // 2 + 1, BAND_MAX + 1, jnp.int32)
    counts = jnp.concatenate([jnp.full((1,), BAND_MAX, jnp.int32), second])
    return jnp.stack([starts, counts], axis=1).astype(jnp.int32)


def draw_far_list(key, part):
    key_row = jax.random.fold_in(key, 31)
    key_col = jax.random.fold_in(key, 32)
    key_band = jax.random.fold_in(key, 33)
    shape = (GRPS, SEGS, SEGS, CAP)
    rows = jax.random.randint(key_row, shape, 0, BLK_DEV, jnp.int32)
    cols = jax.random.randint(key_col, shape, 0, BLK_DEV, jnp.int32)
    bands = jax.random.randint(key_band, shape, 0, 2, jnp.int32)
    return jnp.stack([rows, cols, bands], axis=-1)


def draw_far_count(key, part):
    key_base = jax.random.fold_in(key, 41)
    key_full = jax.random.fold_in(key, 42)
    shape = (GRPS, SEGS, SEGS)
    base = jax.random.randint(key_base, shape, 0, CAP + 1, jnp.int32)
    owner = jax.lax.broadcasted_iota(jnp.int32, shape, 1)
    source = jax.lax.broadcasted_iota(jnp.int32, shape, 2)
    pick = jax.random.randint(key_full, (GRPS, SEGS), 0, SEGS - 1, jnp.int32)
    owner_two = jax.lax.broadcasted_iota(jnp.int32, (GRPS, SEGS), 1)
    pick = pick + (pick >= owner_two).astype(jnp.int32)
    full = source == pick[:, :, None]
    counts = jnp.where(full, CAP, base)
    return jnp.where(owner == source, 0, counts).astype(jnp.int32)


def setup_inputs(seed: int = 0) -> dict:
    keys = jax.random.split(jax.random.key(seed), 5)
    return {
        "spectra": draw_spectra(jax.random.fold_in(keys[4], 71), 0),
        "band_bins": draw_band_bins(jax.random.fold_in(keys[4], 71), 0),
        "far_list": draw_far_list(jax.random.fold_in(keys[4], 71), 0),
        "far_count": draw_far_count(jax.random.fold_in(keys[4], 71), 0),
    }


HIGH = lax.Precision.HIGHEST

def whiten(spectra):
    values = spectra.astype(jnp.float32)
    power = lax.optimization_barrier(jnp.sum(values * values, axis=(0, 1)))
    bins = jnp.arange(F)
    window = (jnp.abs(bins[:, None] - bins[None, :]) <= SMOOTH).astype(jnp.float32)
    totals = lax.optimization_barrier(jnp.sum(window, axis=1)) * W
    level = jnp.dot(window, power, precision=HIGH, preferred_element_type=jnp.float32) / totals[:, None]
    return (values * lax.rsqrt(level + 1e-06)[None, None]).astype(jnp.bfloat16)

def band_operands(white, band_bins):
    cols = []
    ops = []
    for band in range(2):
        piece = lax.dynamic_slice_in_dim(white, band_bins[band, 0], BAND_MAX, 2)
        live = (jnp.arange(BAND_MAX) < band_bins[band, 1]).astype(jnp.bfloat16)
        rows = piece * live[None, None, :, None]
        twisted = jnp.stack([rows[:, 1], -rows[:, 0]], axis=1)
        cols.append(piece)
        ops.append(jnp.stack([rows, twisted], axis=0))
    scales = lax.rsqrt((W * band_bins[:, 1]).astype(jnp.float32))
    return (jnp.stack(cols), jnp.stack(ops), scales)

def reference(spectra, band_bins, far_list, far_count):
    white = whiten(spectra)
    band_cols, row_ops, scales = band_operands(white, band_bins)
    group_cols = band_cols.reshape(2, W, 2, BAND_MAX, SEGS, GCH)
    group_ops = row_ops.reshape(2, 2, W, 2, BAND_MAX, SEGS, GCH)

    def one_group(index):
        cols_here = lax.dynamic_index_in_dim(group_cols, index, 4, keepdims=False).astype(jnp.float32)
        ops_here = lax.dynamic_index_in_dim(group_ops, index, 5, keepdims=False).astype(jnp.float32)
        prod = jnp.einsum('bowpfr,bwpfk->bork', ops_here, cols_here)
        return (prod * scales[:, None, None, None]).astype(jnp.bfloat16)
    near = lax.map(one_group, jnp.arange(SEGS, dtype=jnp.int32))
    near_corr = jnp.transpose(near, (1, 2, 0, 3, 4)).reshape(2, 2, NCH, GCH)
    lists = jnp.transpose(far_list, (1, 0, 2, 3, 4))
    table = jnp.transpose(far_count, (1, 0, 2))
    shape = (SEGS, GRPS, SEGS, CAP)
    owner = lax.broadcasted_iota(jnp.int32, shape, 0)
    member = lax.broadcasted_iota(jnp.int32, shape, 1)
    source = lax.broadcasted_iota(jnp.int32, shape, 2)
    slot = lax.broadcasted_iota(jnp.int32, shape, 3)
    row_block = (owner * GRPS + member) * BLK_DEV + lists[..., 0]
    col_block = (source * GRPS + member) * BLK_DEV + lists[..., 1]
    band_pick = lists[..., 2]
    alive = (slot < table[..., None]).astype(jnp.float32)
    per_dev = SEGS * CAP
    row_block = row_block.reshape(DEVICES, per_dev)
    col_block = col_block.reshape(DEVICES, per_dev)
    band_pick = band_pick.reshape(DEVICES, per_dev)
    alive = alive.reshape(DEVICES, per_dev)
    block_cols = band_cols.reshape(2, W, 2, BAND_MAX, NBLK, BLOCK)
    block_ops = row_ops.reshape(2, 2, W, 2, BAND_MAX, NBLK, BLOCK)

    def one_owner(inputs):
        rows_i, cols_i, bands_i, alive_i = inputs
        chosen_cols = block_cols[bands_i, :, :, :, cols_i, :].astype(jnp.float32)
        chosen_ops = block_ops[bands_i, :, :, :, :, rows_i, :].astype(jnp.float32)
        prod = jnp.einsum('cowpfr,cwpfk->cork', chosen_ops, chosen_cols)
        factor = scales[bands_i] * alive_i
        return (prod * factor[:, None, None, None]).astype(jnp.bfloat16)
    far = lax.map(one_owner, (row_block, col_block, band_pick, alive))
    far_corr = far.reshape(SEGS, GRPS, SEGS, CAP, 2, BLOCK, BLOCK)
    return (near_corr, far_corr)
```

```python
import functools
import math

import jax
import jax.numpy as jnp
from jax import lax
from jax.experimental import pallas as pl
from jax.experimental.pallas import tpu as pltpu
from jax.sharding import PartitionSpec as P

W = 8
F = 128
BAND_MAX = 48
SMOOTH = 4
BLOCK = 128
BLK_DEV = 3
DEPTH = W * 2 * BAND_MAX
PIECES = 2 * BLK_DEV
LEVELS = 4
CORES = 2


HIGH = lax.Precision.HIGHEST
MESH = pl.DeviceIdType.MESH


def whiten(m, bins, spec, cols):
    power = jnp.zeros((F, BLOCK), jnp.float32)
    for w in range(W):
        for p in range(2):
            values = spec[m % 2, w, p].astype(jnp.float32)
            power = power + values * values
    f = lax.broadcasted_iota(jnp.int32, (F, F), 0)
    g = lax.broadcasted_iota(jnp.int32, (F, F), 1)
    window = jnp.where(jnp.abs(f - g) <= SMOOTH, 1.0, 0.0).astype(jnp.float32)
    totals = jnp.sum(window, axis=1, keepdims=True) * W
    level = jnp.dot(window, power, precision=HIGH, preferred_element_type=jnp.float32) / totals
    gain = lax.rsqrt(level + 1e-06)
    ahead = jnp.full((BAND_MAX, BLOCK), bins[0, 0], jnp.int32) == 0
    for p in range(2):
        for w in range(W):
            at = slice((p * W + w) * BAND_MAX, (p * W + w + 1) * BAND_MAX)
            low = spec[m % 2, w, p, :BAND_MAX].astype(jnp.float32) * gain[:BAND_MAX]
            high = spec[m % 2, w, p, F - BAND_MAX :].astype(jnp.float32) * gain[F - BAND_MAX :]
            cols[m * 2, at] = jnp.where(ahead, low, high).astype(jnp.bfloat16)
            cols[m * 2 + 1, at] = jnp.where(ahead, high, low).astype(jnp.bfloat16)


class Gather:
    def __init__(self, axis, high, low, own, buf, send, recv):
        self.axis, self.high, self.low = axis, high, low
        self.own, self.buf, self.send, self.recv = own, buf, send, recv
        self.me = lax.axis_index(axis)
        self.p, self.l = lax.div(self.me, low), lax.rem(self.me, low)
        p, l = self.p, self.l
        self.dirs = [
            (p + 1 < high, self.me + low),
            (p > 0, self.me - low),
            (l + 1 < low, self.me + 1),
            (l > 0, self.me - 1),
        ]
        if high == 1:
            self.dirs[0] = self.dirs[1] = None
        if low == 1:
            self.dirs[2] = self.dirs[3] = None
        self.closing = False

    def greet(self, barrier):
        for entry in self.dirs:
            if entry is not None:

                @pl.when(entry[0])
                def _():
                    pl.semaphore_signal(
                        barrier, inc=1, device_id={self.axis: entry[1]}, device_id_type=MESH
                    )

    def peers(self):
        return sum(jnp.where(entry[0], 1, 0) for entry in self.dirs if entry is not None)

    def copy(self, way, src, q, own):
        return pltpu.make_async_remote_copy(
            src_ref=self.own.at[q] if own else self.buf.at[src, q],
            dst_ref=self.buf.at[src, q],
            send_sem=self.send.at[way, src, q],
            recv_sem=self.recv.at[src, q],
            device_id={self.axis: self.dirs[way][1]},
            device_id_type=MESH,
        )

    def pass_on(self, ways, src, q, own=False):
        for way in ways:
            if self.dirs[way] is not None:

                @pl.when(self.dirs[way][0])
                def _():
                    piece = self.copy(way, src, q, own)
                    if self.closing:
                        piece.wait_send()
                    else:
                        piece.start()

    def arrive(self, there, src, q, ways, use):
        @pl.when(there)
        def _():
            if not self.closing:
                pltpu.make_async_copy(
                    self.buf.at[src, q], self.buf.at[src, q], self.recv.at[src, q]
                ).wait()
            self.pass_on(ways, src, q)
            if use is not None and not self.closing:
                use(src, q)

    def start(self, q):
        self.pass_on((0, 1, 2, 3), self.me, q, own=True)

    def step(self, st, q, use, low_first=False):
        p, l, low = self.p, self.l, self.low
        turn = () if low_first else (2, 3)
        if 0 < st < self.high:
            self.arrive(p - st >= 0, (p - st) * low + l, q, (0,) + turn, use)
            self.arrive(p + st < self.high, (p + st) * low + l, q, (1,) + turn, use)
        d = st - 1
        if not 0 <= d < self.high:
            return
        for far, way in [(p, None)] if d == 0 else [(p - d, 0), (p + d, 1)]:
            inside = (far >= 0) & (far < self.high)
            for e in range(1, low):
                for there, other, on in ((l - e >= 0, l - e, 2), (l + e < low, l + e, 3)):
                    if not low_first:
                        ways = (on,)
                    elif d == 0:
                        ways = (0, 1, on)
                    else:
                        ways = (way,)
                    self.arrive(inside & there, far * low + other, q, ways, use)


class Line:
    def __init__(self, low, own, bufs, send, recv):
        self.low, self.own, self.bufs, self.send, self.recv = low, own, bufs, send, recv
        self.me = lax.axis_index("seg")
        self.z = lax.div(self.me, low)
        self.closing = False

    def slot(self, d, way):
        return d if d > 1 else 1 - way

    def buf(self, d, way):
        return self.bufs[self.slot(d, way)]

    def move(self, way, d, q):
        at = self.slot(d + 1, way)
        piece = pltpu.make_async_remote_copy(
            src_ref=self.buf(d, way).at[q] if d else self.own.at[q],
            dst_ref=self.bufs[at].at[q],
            send_sem=self.send.at[way, d, q],
            recv_sem=self.recv.at[at, q],
            device_id={"seg": self.me + (self.low if way else -self.low)},
            device_id_type=MESH,
        )
        if self.closing:
            piece.wait_send()
        else:
            piece.start()

    def start(self, q):
        z = self.z

        @pl.when((z + 1 < LEVELS) & (z != LEVELS - 2))
        def _():
            self.move(1, 0, q)

        @pl.when((z > 0) & (z != 1))
        def _():
            self.move(0, 0, q)

    def there(self, d):
        z = self.z
        left, right = z - d >= 0, z + d < LEVELS
        if d == 1:
            left, right = left & (z != LEVELS - 1), right & (z != 0)
        return ((left, z - d, z + 1 < LEVELS, 1), (right, z + d, z > 0, 0))

    def arrive(self, d, q):
        for here, _, on, way in self.there(d):

            @pl.when(here)
            def _():
                if not self.closing:
                    at = self.slot(d, way)
                    piece = self.bufs[at].at[q]
                    pltpu.make_async_copy(piece, piece, self.recv.at[at, q]).wait()

                if d + 1 < LEVELS:

                    @pl.when(on)
                    def _():
                        self.move(way, d, q)


def kernel(
    nseg, ngrp, bins, lists, counts, spectra, near, far,
    spec, cols, left, right, two, three, side, grp_buf, ops, stage, end_stage,
    spec_sem, line_send, line_recv, side_send, side_recv, grp_send, grp_recv,
    far_send, end_send, far_recv, move,
):
    low = nseg // LEVELS
    slots = far.shape[1]
    line = Line(low, cols, (left, right, two, three), line_send, line_recv)
    grp = Gather("grp", ngrp // CORES, CORES, cols, grp_buf, grp_send, grp_recv)
    me, z = line.me, line.z
    y = lax.rem(me, low)
    mates = [lax.rem(y + e, low) for e in range(1, low)]
    is_end = (z == 0) | (z == LEVELS - 1)
    inner = (z == 1) | (z == LEVELS - 2)
    end = jnp.where(z == 1, 0, LEVELS - 1)
    beside = jnp.where(z == 0, 1, LEVELS - 2)

    def load(m):
        return pltpu.make_async_copy(
            spectra.at[:, :, :, m * BLOCK : (m + 1) * BLOCK], spec.at[m % 2], spec_sem.at[m % 2]
        )

    load(0).start()
    load(1).start()

    barrier = pltpu.get_barrier_semaphore()

    def greet(seg):
        pl.semaphore_signal(barrier, inc=1, device_id={"seg": seg}, device_id_type=MESH)

    for on, seg in ((z + 1 < LEVELS, me + low), (z > 0, me - low)):

        @pl.when(on)
        def _():
            greet(seg)

    for mate in mates:
        greet(z * low + mate)
    grp.greet(barrier)

    def side_copy(e, q):
        return pltpu.make_async_remote_copy(
            src_ref=cols.at[q],
            dst_ref=side.at[y, q],
            send_sem=side_send.at[e, q],
            recv_sem=side_recv.at[y, q],
            device_id={"seg": z * low + mates[e]},
            device_id_type=MESH,
        )

    def begin(q):
        line.start(q)
        for e in range(low - 1):
            if line.closing:
                side_copy(e, q).wait_send()
            else:
                side_copy(e, q).start()
        grp.start(q)

    def loop(fn, count=PIECES):
        def step(q, carry):
            fn(q)
            return carry

        lax.fori_loop(0, count, step, 0)

    for m in range(BLK_DEV):
        load(m).wait()
        whiten(m, bins, spec, cols)
        if m + 2 < BLK_DEV:
            load(m + 2).start()
        if m == 0:
            inner_peers = jnp.where(z + 1 < LEVELS, 1, 0) + jnp.where(z > 0, 1, 0)
            pl.semaphore_wait(barrier, inner_peers + (low - 1) + grp.peers())
        begin(2 * m)
        begin(2 * m + 1)

    own = pltpu.make_async_copy(cols, side.at[y], move)
    own.start()

    half = DEPTH // 2

    def operands(slot, q, piece):
        band = lax.rem(q, 2)
        bin_of = lax.rem(lax.broadcasted_iota(jnp.int32, (1, DEPTH), 1), BAND_MAX)
        live = jnp.where(bin_of < bins[band, 1], 1.0, 0.0).astype(jnp.float32)
        rows = jnp.transpose(piece.astype(jnp.float32)) * live
        ops[slot, q, :BLOCK] = rows.astype(jnp.bfloat16)
        ops[slot, q, BLOCK:, :half] = rows[:, half:].astype(jnp.bfloat16)
        ops[slot, q, BLOCK:, half:] = (-rows[:, :half]).astype(jnp.bfloat16)

    loop(lambda q: operands(y, q, cols[q]))

    def scale(band):
        return lax.rsqrt(jnp.full((1, BLOCK), W * bins[band, 1], jnp.int32).astype(jnp.float32))

    def near_from(piece, src, q):
        m, band = lax.div(q, 2), lax.rem(q, 2)
        at = pl.ds(pl.multiple_of(src * (BLK_DEV * BLOCK) + m * BLOCK, BLOCK), BLOCK)
        for i in range(BLK_DEV):
            prod = jnp.dot(ops[y, i * 2 + band], piece, preferred_element_type=jnp.float32)
            prod = (prod * scale(band)).astype(jnp.bfloat16)
            near[band, 0, i * BLOCK : (i + 1) * BLOCK, at] = prod[:BLOCK]
            near[band, 1, i * BLOCK : (i + 1) * BLOCK, at] = prod[BLOCK:]

    def use_near(src, q):
        near_from(grp_buf[src, q], src, q)

    loop(lambda q: near_from(cols[q], grp.me, q))

    def pair(owner, slot, src, t, dst, c):
        i, m, band = lists[owner, 0, c, t], lists[owner, 1, c, t], lists[owner, 2, c, t]
        factor = jnp.where(c < counts[owner, t], scale(band), 0.0)
        prod = jnp.dot(
            ops[slot, i * 2 + band], src[m * 2 + band], preferred_element_type=jnp.float32
        )
        prod = (prod * factor).astype(jnp.bfloat16)
        dst[c, 0] = prod[:BLOCK]
        dst[c, 1] = prod[BLOCK:]

    def level_pairs(buf, src, c):
        t = src * low + y
        pair(me, y, buf, t, far.at[t], c)
        for mate in mates:
            pair(z * low + mate, mate, buf, t, stage.at[mate, src], c)

    def hand_over(src):
        for mate in mates:
            piece = pltpu.make_async_remote_copy(
                src_ref=stage.at[mate, src],
                dst_ref=far.at[src * low + y],
                send_sem=far_send.at[mate, src],
                recv_sem=far_recv.at[src * low + y],
                device_id={"seg": z * low + mate},
                device_id_type=MESH,
            )
            if line.closing:
                piece.wait_send()
            else:
                piece.start()

    def end_copy(other):
        return pltpu.make_async_remote_copy(
            src_ref=end_stage.at[other],
            dst_ref=far.at[z * low + other],
            send_sem=end_send.at[other],
            recv_sem=far_recv.at[z * low + other],
            device_id={"seg": end * low + y},
            device_id_type=MESH,
        )

    def for_end():
        for at, buf in ((1, left), (LEVELS - 2, right)):

            @pl.when(z == at)
            def _():
                loop(lambda q: operands(low, q, buf[q]))

        @pl.when(inner)
        def _():
            for other in [y] + mates:
                t = z * low + other
                loop(
                    lambda c: pair(end * low + y, low, side.at[other], t, end_stage.at[other], c),
                    slots,
                )
                end_copy(other).start()

    def first(q):
        line.arrive(1, q)
        grp.step(1, q, None if grp.closing else use_near)
        if not line.closing:
            for mate in mates:
                pltpu.make_async_copy(
                    side.at[mate, q], side.at[mate, q], side_recv.at[mate, q]
                ).wait()
                operands(mate, q, side[mate, q])

    def second(q):
        line.arrive(2, q)
        grp.step(2, q, None if grp.closing else use_near)
        if not line.closing:

            @pl.when(q < slots)
            def _():
                for mate in mates:
                    t = z * low + mate
                    pair(me, y, side.at[mate], t, far.at[t], q)
                for here, src, _, way in line.there(1):

                    @pl.when(here)
                    def _():
                        level_pairs(line.buf(1, way), src, q)

                        @pl.when(q == slots - 1)
                        def _():
                            hand_over(src)

    def later(d):
        def step(q):
            if d < LEVELS:
                line.arrive(d, q)
            grp.step(d, q, None if grp.closing else use_near)

        loop(step)

    def after(d):
        for here, src, _, way in line.there(d):

            @pl.when(here)
            def _():
                if not line.closing:
                    loop(lambda c: level_pairs(line.buf(d, way), src, c), slots)
                hand_over(src)

    loop(first)
    own.wait()
    far[me] = jnp.zeros(far.shape[1:], far.dtype)
    for_end()
    loop(second)
    after(2)
    for d in range(3, max(LEVELS, grp.high + 1)):
        later(d)
        if d < LEVELS:
            after(d)

    line.closing = grp.closing = True
    loop(begin)
    loop(first)
    after(1)
    loop(second)
    after(2)
    for d in range(3, max(LEVELS, grp.high + 1)):
        later(d)
        if d < LEVELS:
            after(d)

    @pl.when(inner)
    def _():
        for other in [y] + mates:
            end_copy(other).wait_send()

    def landed(t):
        tz, ty = lax.div(t, low), lax.rem(t, low)

        @pl.when(((ty != y) & (tz != z)) | (is_end & (tz == beside) & (ty == y)))
        def _():
            pltpu.make_async_copy(far.at[t], far.at[t], far_recv.at[t]).wait()

    loop(landed, nseg)


def body(nseg, ngrp, spectra, band_bins, far_list, far_count):
    slots = far_list.shape[3]
    low = nseg // LEVELS
    smem = pl.BlockSpec(memory_space=pltpu.SMEM)
    whole = pl.BlockSpec(memory_space=pltpu.VMEM)
    sems = pltpu.SemaphoreType.DMA
    half = jnp.bfloat16
    near = jax.ShapeDtypeStruct((2, 2, BLK_DEV * BLOCK, ngrp * BLK_DEV * BLOCK), half)
    far = jax.ShapeDtypeStruct((nseg, slots, 2, BLOCK, BLOCK), half)
    buffers = [
        pltpu.VMEM((2, W, 2, F, BLOCK), half),
        pltpu.VMEM((PIECES, DEPTH, BLOCK), half),
        pltpu.VMEM((PIECES, DEPTH, BLOCK), half),
        pltpu.VMEM((PIECES, DEPTH, BLOCK), half),
        pltpu.VMEM((PIECES, DEPTH, BLOCK), half),
        pltpu.VMEM((PIECES, DEPTH, BLOCK), half),
        pltpu.VMEM((low, PIECES, DEPTH, BLOCK), half),
        pltpu.VMEM((ngrp, PIECES, DEPTH, BLOCK), half),
        pltpu.VMEM((low + 1, PIECES, 2 * BLOCK, DEPTH), half),
        pltpu.VMEM((low, LEVELS, slots, 2, BLOCK, BLOCK), half),
        pltpu.VMEM((low, slots, 2, BLOCK, BLOCK), half),
    ]
    vmem = sum(math.prod(a.shape) * 2 for a in buffers + [near, far]) + 2 * 1024 * 1024
    near, far = pl.pallas_call(
        functools.partial(kernel, nseg, ngrp),
        out_shape=(near, far),
        in_specs=[smem, smem, smem, pl.BlockSpec(memory_space=pl.ANY)],
        out_specs=(whole, whole),
        scratch_shapes=buffers
        + [
            sems((2,)),
            sems((2, LEVELS, PIECES)),
            sems((LEVELS, PIECES)),
            sems((low, PIECES)),
            sems((low, PIECES)),
            sems((4, ngrp, PIECES)),
            sems((ngrp, PIECES)),
            sems((low, LEVELS)),
            sems((low,)),
            sems((nseg,)),
            sems,
        ],
        compiler_params=pltpu.CompilerParams(
            collective_id=0, has_side_effects=True, vmem_limit_bytes=vmem
        ),
    )(band_bins, jnp.transpose(far_list[0], (0, 3, 2, 1)), far_count[0], spectra)
    return (near, far[None, None])


def solution(mesh):
    placed = (
        P(None, None, None, ("seg", "grp")),
        P(),
        P("grp", None, None, None, None),
        P("grp", None, None),
    )
    return jax.shard_map(
        functools.partial(body, mesh.shape["seg"], mesh.shape["grp"]),
        mesh=mesh,
        in_specs=placed,
        out_specs=(
            P(None, None, ("seg", "grp"), None),
            P("seg", "grp", None, None, None, None, None),
        ),
        check_vma=False,
    )
```

```python
import functools
import math

import jax
import jax.numpy as jnp
from jax import lax
from jax.experimental import pallas as pl
from jax.experimental.pallas import tpu as pltpu
from jax.sharding import PartitionSpec as P

W = 8
F = 128
BAND_MAX = 48
SMOOTH = 4
BLOCK = 128
BLK_DEV = 3
DEPTH = W * 2 * BAND_MAX
PIECES = 2 * BLK_DEV
LEVELS = 4
PARTS = 2
CORES = 2


HIGH = lax.Precision.HIGHEST
MESH = pl.DeviceIdType.MESH


def whiten(m, bins, spec, cols):
    power = jnp.zeros((F, BLOCK), jnp.float32)
    for w in range(W):
        for p in range(2):
            values = spec[m % 2, w, p].astype(jnp.float32)
            power = power + values * values
    f = lax.broadcasted_iota(jnp.int32, (F, F), 0)
    g = lax.broadcasted_iota(jnp.int32, (F, F), 1)
    window = jnp.where(jnp.abs(f - g) <= SMOOTH, 1.0, 0.0).astype(jnp.float32)
    totals = jnp.sum(window, axis=1, keepdims=True) * W
    level = jnp.dot(window, power, precision=HIGH, preferred_element_type=jnp.float32) / totals
    gain = lax.rsqrt(level + 1e-06)
    ahead = jnp.full((BAND_MAX, BLOCK), bins[0, 0], jnp.int32) == 0
    for p in range(2):
        for w in range(W):
            at = slice((p * W + w) * BAND_MAX, (p * W + w + 1) * BAND_MAX)
            low = spec[m % 2, w, p, :BAND_MAX].astype(jnp.float32) * gain[:BAND_MAX]
            high = spec[m % 2, w, p, F - BAND_MAX :].astype(jnp.float32) * gain[F - BAND_MAX :]
            cols[m * 2, at] = jnp.where(ahead, low, high).astype(jnp.bfloat16)
            cols[m * 2 + 1, at] = jnp.where(ahead, high, low).astype(jnp.bfloat16)


class Gather:
    def __init__(self, axis, high, low, own, buf, send, recv):
        self.axis, self.high, self.low = axis, high, low
        self.own, self.buf, self.send, self.recv = own, buf, send, recv
        self.me = lax.axis_index(axis)
        self.p, self.l = lax.div(self.me, low), lax.rem(self.me, low)
        p, l = self.p, self.l
        self.dirs = [
            (p + 1 < high, self.me + low),
            (p > 0, self.me - low),
            (l + 1 < low, self.me + 1),
            (l > 0, self.me - 1),
        ]
        if high == 1:
            self.dirs[0] = self.dirs[1] = None
        if low == 1:
            self.dirs[2] = self.dirs[3] = None
        self.closing = False

    def greet(self, barrier):
        for entry in self.dirs:
            if entry is not None:

                @pl.when(entry[0])
                def _():
                    pl.semaphore_signal(
                        barrier, inc=1, device_id={self.axis: entry[1]}, device_id_type=MESH
                    )

    def peers(self):
        return sum(jnp.where(entry[0], 1, 0) for entry in self.dirs if entry is not None)

    def copy(self, way, src, q, own):
        return pltpu.make_async_remote_copy(
            src_ref=self.own.at[q] if own else self.buf.at[src, q],
            dst_ref=self.buf.at[src, q],
            send_sem=self.send.at[way, src, q],
            recv_sem=self.recv.at[src, q],
            device_id={self.axis: self.dirs[way][1]},
            device_id_type=MESH,
        )

    def pass_on(self, ways, src, q, own=False):
        for way in ways:
            if self.dirs[way] is not None:

                @pl.when(self.dirs[way][0])
                def _():
                    piece = self.copy(way, src, q, own)
                    if self.closing:
                        piece.wait_send()
                    else:
                        piece.start()

    def arrive(self, there, src, q, ways, use):
        @pl.when(there)
        def _():
            if not self.closing:
                pltpu.make_async_copy(
                    self.buf.at[src, q], self.buf.at[src, q], self.recv.at[src, q]
                ).wait()
            self.pass_on(ways, src, q)
            if use is not None and not self.closing:
                use(src, q)

    def start(self, q):
        self.pass_on((0, 1, 2, 3), self.me, q, own=True)

    def step(self, st, q, use, low_first=False):
        p, l, low = self.p, self.l, self.low
        turn = () if low_first else (2, 3)
        if 0 < st < self.high:
            self.arrive(p - st >= 0, (p - st) * low + l, q, (0,) + turn, use)
            self.arrive(p + st < self.high, (p + st) * low + l, q, (1,) + turn, use)
        d = st - 1
        if not 0 <= d < self.high:
            return
        for far, way in [(p, None)] if d == 0 else [(p - d, 0), (p + d, 1)]:
            inside = (far >= 0) & (far < self.high)
            for e in range(1, low):
                for there, other, on in ((l - e >= 0, l - e, 2), (l + e < low, l + e, 3)):
                    if not low_first:
                        ways = (on,)
                    elif d == 0:
                        ways = (0, 1, on)
                    else:
                        ways = (way,)
                    self.arrive(inside & there, far * low + other, q, ways, use)


def part_rows(part):
    return pl.ds(part * (DEPTH // PARTS), DEPTH // PARTS)


class Line:
    def __init__(self, low, own, bufs, send, recv):
        self.low, self.own, self.bufs, self.send, self.recv = low, own, bufs, send, recv
        self.me = lax.axis_index("seg")
        self.z = lax.div(self.me, low)
        self.closing = False

    def slot(self, d, way):
        return d if d > 1 else 1 - way

    def buf(self, d, way):
        return self.bufs[self.slot(d, way)]

    def move(self, way, d, q, part):
        at = self.slot(d + 1, way)
        rows = part_rows(part)
        piece = pltpu.make_async_remote_copy(
            src_ref=(self.buf(d, way) if d else self.own).at[q, rows],
            dst_ref=self.bufs[at].at[q, rows],
            send_sem=self.send.at[way, d, q, part],
            recv_sem=self.recv.at[at, q, part],
            device_id={"seg": self.me + (self.low if way else -self.low)},
            device_id_type=MESH,
        )
        if self.closing:
            piece.wait_send()
        else:
            piece.start()

    def start(self, q):
        z = self.z

        @pl.when((z + 1 < LEVELS) & (z != LEVELS - 2))
        def _():
            for part in range(PARTS):
                self.move(1, 0, q, part)

        @pl.when((z > 0) & (z != 1))
        def _():
            for part in range(PARTS):
                self.move(0, 0, q, part)

    def there(self, d):
        z = self.z
        left, right = z - d >= 0, z + d < LEVELS
        if d == 1:
            left, right = left & (z != LEVELS - 1), right & (z != 0)
        return ((left, z - d, z + 1 < LEVELS, 1), (right, z + d, z > 0, 0))

    def arrive(self, d, q, then=None):
        for part in range(PARTS):
            for here, _, on, way in self.there(d):

                @pl.when(here)
                def _():
                    if not self.closing:
                        at = self.slot(d, way)
                        piece = self.bufs[at].at[q, part_rows(part)]
                        pltpu.make_async_copy(piece, piece, self.recv.at[at, q, part]).wait()

                    if d + 1 < LEVELS:

                        @pl.when(on)
                        def _():
                            self.move(way, d, q, part)

                    if then is not None:
                        then(q, part)


def kernel(
    nseg, ngrp, bins_in, lists_in, counts_in, spectra, near_out, far_out,
    bins, lists, counts, near, far, spec, cols, left, right, two, three, side, grp_buf, ops, stage, end_stage,
    spec_sem, line_send, line_recv, side_send, side_recv, grp_send, grp_recv,
    far_send, end_send, far_recv, pass_send, pass_recv, small_sem, out_sem, move, near_sem,
):
    low = nseg // LEVELS
    slots = far.shape[1]
    line = Line(low, cols, (left, right, two, three), line_send, line_recv)
    grp = Gather("grp", ngrp // CORES, CORES, cols, grp_buf, grp_send, grp_recv)
    me, z = line.me, line.z
    y = lax.rem(me, low)
    mates = [lax.rem(y + e, low) for e in range(1, low)]
    before = lax.rem(y + low - 1, low)
    is_end = (z == 0) | (z == LEVELS - 1)
    inner = (z == 1) | (z == LEVELS - 2)
    end = jnp.where(z == 1, 0, LEVELS - 1)
    beside = jnp.where(z == 0, 1, LEVELS - 2)

    def load(m):
        return pltpu.make_async_copy(
            spectra.at[:, :, :, m * BLOCK : (m + 1) * BLOCK], spec.at[m % 2], spec_sem.at[m % 2]
        )

    small = [
        pltpu.make_async_copy(a, b, small_sem.at[k])
        for k, (a, b) in enumerate(((bins_in, bins), (lists_in, lists), (counts_in, counts)))
    ]
    for copy in small:
        copy.start()
    load(0).start()
    load(1).start()

    barrier = pltpu.get_barrier_semaphore()

    def greet(seg):
        pl.semaphore_signal(barrier, inc=1, device_id={"seg": seg}, device_id_type=MESH)

    for on, seg in ((z + 1 < LEVELS, me + low), (z > 0, me - low)):

        @pl.when(on)
        def _():
            greet(seg)

    for mate in mates:
        greet(z * low + mate)
    grp.greet(barrier)

    def side_copy(e, q):
        return pltpu.make_async_remote_copy(
            src_ref=cols.at[q],
            dst_ref=side.at[y, q],
            send_sem=side_send.at[e, q],
            recv_sem=side_recv.at[y, q],
            device_id={"seg": z * low + mates[e]},
            device_id_type=MESH,
        )

    def begin(q):
        line.start(q)
        for e in range(low - 1):
            if line.closing:
                side_copy(e, q).wait_send()
            else:
                side_copy(e, q).start()
        grp.start(q)

    def loop(fn, count=PIECES):
        def step(q, carry):
            fn(q)
            return carry

        lax.fori_loop(0, count, step, 0)

    for copy in small:
        copy.wait()
    for m in range(BLK_DEV):
        load(m).wait()
        whiten(m, bins, spec, cols)
        if m + 2 < BLK_DEV:
            load(m + 2).start()
        if m == 0:
            inner_peers = jnp.where(z + 1 < LEVELS, 1, 0) + jnp.where(z > 0, 1, 0)
            pl.semaphore_wait(barrier, inner_peers + (low - 1) + grp.peers())
        begin(2 * m)
        begin(2 * m + 1)

    own = pltpu.make_async_copy(cols, side.at[y], move)
    own.start()

    half = DEPTH // 2

    def operands(slot, q, piece):
        band = lax.rem(q, 2)
        bin_of = lax.rem(lax.broadcasted_iota(jnp.int32, (1, DEPTH), 1), BAND_MAX)
        live = jnp.where(bin_of < bins[band, 1], 1.0, 0.0).astype(jnp.float32)
        rows = jnp.transpose(piece.astype(jnp.float32)) * live
        ops[slot, q, :BLOCK] = rows.astype(jnp.bfloat16)
        ops[slot, q, BLOCK:, :half] = rows[:, half:].astype(jnp.bfloat16)
        ops[slot, q, BLOCK:, half:] = (-rows[:, :half]).astype(jnp.bfloat16)

    loop(lambda q: operands(y, q, cols[q]))

    def scale(band):
        return lax.rsqrt(jnp.full((1, BLOCK), W * bins[band, 1], jnp.int32).astype(jnp.float32))

    def near_from(piece, src, q):
        m, band = lax.div(q, 2), lax.rem(q, 2)
        at = pl.ds(pl.multiple_of(src * (BLK_DEV * BLOCK) + m * BLOCK, BLOCK), BLOCK)
        for i in range(BLK_DEV):
            prod = jnp.dot(ops[y, i * 2 + band], piece, preferred_element_type=jnp.float32)
            prod = (prod * scale(band)).astype(jnp.bfloat16)
            near[band, 0, i * BLOCK : (i + 1) * BLOCK, at] = prod[:BLOCK]
            near[band, 1, i * BLOCK : (i + 1) * BLOCK, at] = prod[BLOCK:]

    def use_near(src, q):
        near_from(grp_buf[src, q], src, q)

    loop(lambda q: near_from(cols[q], grp.me, q))

    def pair(owner, slot, src, t, dst, c):
        i, m, band = lists[owner, 0, c, t], lists[owner, 1, c, t], lists[owner, 2, c, t]
        factor = jnp.where(c < counts[owner, t], scale(band), 0.0)
        prod = jnp.dot(
            ops[slot, i * 2 + band], src[m * 2 + band], preferred_element_type=jnp.float32
        )
        prod = (prod * factor).astype(jnp.bfloat16)
        dst[c, 0] = prod[:BLOCK]
        dst[c, 1] = prod[BLOCK:]

    def pass_on(q, part):
        rows = part_rows(part)
        piece = pltpu.make_async_remote_copy(
            src_ref=three.at[q, rows],
            dst_ref=left.at[q, rows],
            send_sem=pass_send.at[q, part],
            recv_sem=pass_recv.at[q, part],
            device_id={"seg": z * low + mates[0]},
            device_id_type=MESH,
        )
        if line.closing:
            piece.wait_send()
        else:
            piece.start()

    def passed(q):
        for part in range(PARTS):
            piece = left.at[q, part_rows(part)]
            pltpu.make_async_copy(piece, piece, pass_recv.at[q, part]).wait()

    def level_pairs(buf, src, c, others):
        t = src * low + y
        pair(me, y, buf, t, far.at[t], c)
        for mate in others:
            pair(z * low + mate, mate, buf, t, stage.at[mate, src], c)

    def hand_over(src, others):
        for mate in others:
            piece = pltpu.make_async_remote_copy(
                src_ref=stage.at[mate, src],
                dst_ref=far.at[src * low + y],
                send_sem=far_send.at[mate, src],
                recv_sem=far_recv.at[src * low + y],
                device_id={"seg": z * low + mate},
                device_id_type=MESH,
            )
            if line.closing:
                piece.wait_send()
            else:
                piece.start()

    def end_copy(other):
        return pltpu.make_async_remote_copy(
            src_ref=end_stage.at[other],
            dst_ref=far.at[z * low + other],
            send_sem=end_send.at[other],
            recv_sem=far_recv.at[z * low + other],
            device_id={"seg": end * low + y},
            device_id_type=MESH,
        )

    def for_end():
        for at, buf in ((1, left), (LEVELS - 2, right)):

            @pl.when(z == at)
            def _():
                loop(lambda q: operands(low, q, buf[q]))

        @pl.when(inner)
        def _():
            for other in [y] + mates:
                t = z * low + other
                loop(
                    lambda c: pair(end * low + y, low, side.at[other], t, end_stage.at[other], c),
                    slots,
                )
                end_copy(other).start()

    def first(q):
        line.arrive(1, q)
        grp.step(1, q, None if grp.closing else use_near)
        if not line.closing:
            for mate in mates:
                pltpu.make_async_copy(
                    side.at[mate, q], side.at[mate, q], side_recv.at[mate, q]
                ).wait()
                operands(mate, q, side[mate, q])

    def second(q):
        line.arrive(2, q)
        grp.step(2, q, None if grp.closing else use_near)
        if not line.closing:

            @pl.when(q < slots)
            def _():
                for mate in mates:
                    t = z * low + mate
                    pair(me, y, side.at[mate], t, far.at[t], q)
                for here, src, _, way in line.there(1):

                    @pl.when(here)
                    def _():
                        level_pairs(line.buf(1, way), src, q, mates)

                        @pl.when(q == slots - 1)
                        def _():
                            hand_over(src, mates)

    def later(d):
        def step(q):
            if d < LEVELS:
                line.arrive(d, q, pass_on if d == LEVELS - 1 else None)
            grp.step(d, q, None if grp.closing else use_near)

        loop(step)

    def after(d):
        last = d == LEVELS - 1
        others = mates[1:] if last else mates
        for here, src, _, way in line.there(d):

            @pl.when(here)
            def _():
                if not line.closing:
                    loop(lambda c: level_pairs(line.buf(d, way), src, c, others), slots)
                hand_over(src, others)
                if last and not line.closing:
                    loop(passed)
                    t = src * low + before
                    loop(lambda c: pair(me, y, left, t, far.at[t], c), slots)

    loop(first)
    own.wait()
    far[me] = jnp.zeros(far.shape[1:], far.dtype)
    for_end()
    loop(second)
    near_copy = pltpu.make_async_copy(near, near_out, near_sem)
    if grp.high < 3:
        near_copy.start()
    after(2)
    for d in range(3, max(LEVELS, grp.high + 1)):
        later(d)
        if d == grp.high:
            near_copy.start()
        if d < LEVELS:
            after(d)

    line.closing = grp.closing = True
    loop(begin)
    loop(first)
    after(1)
    loop(second)
    after(2)
    for d in range(3, max(LEVELS, grp.high + 1)):
        later(d)
        if d < LEVELS:
            after(d)

    @pl.when(inner)
    def _():
        for other in [y] + mates:
            end_copy(other).wait_send()

    def far_copy(t):
        return pltpu.make_async_copy(far.at[t], far_out.at[t], out_sem.at[t])

    def landed(t):
        tz, ty = lax.div(t, low), lax.rem(t, low)

        handed = (ty != y) & (tz != z) & ~(is_end & (tz == LEVELS - 1 - z) & (ty == before))

        @pl.when(handed | (is_end & (tz == beside) & (ty == y)))
        def _():
            pltpu.make_async_copy(far.at[t], far.at[t], far_recv.at[t]).wait()

        far_copy(t).start()

    loop(landed, nseg)
    loop(lambda t: far_copy(t).wait(), nseg)
    near_copy.wait()


def body(nseg, ngrp, spectra, band_bins, far_list, far_count):
    slots = far_list.shape[3]
    low = nseg // LEVELS
    hbm = pl.BlockSpec(memory_space=pl.ANY)
    sems = pltpu.SemaphoreType.DMA
    half = jnp.bfloat16
    small = (band_bins, jnp.transpose(far_list[0], (0, 3, 2, 1)), far_count[0])
    near = jax.ShapeDtypeStruct((2, 2, BLK_DEV * BLOCK, ngrp * BLK_DEV * BLOCK), half)
    far = jax.ShapeDtypeStruct((nseg, slots, 2, BLOCK, BLOCK), half)
    buffers = [
        pltpu.VMEM(near.shape, half),
        pltpu.VMEM(far.shape, half),
        pltpu.VMEM((2, W, 2, F, BLOCK), half),
        pltpu.VMEM((PIECES, DEPTH, BLOCK), half),
        pltpu.VMEM((PIECES, DEPTH, BLOCK), half),
        pltpu.VMEM((PIECES, DEPTH, BLOCK), half),
        pltpu.VMEM((PIECES, DEPTH, BLOCK), half),
        pltpu.VMEM((PIECES, DEPTH, BLOCK), half),
        pltpu.VMEM((low, PIECES, DEPTH, BLOCK), half),
        pltpu.VMEM((ngrp, PIECES, DEPTH, BLOCK), half),
        pltpu.VMEM((low + 1, PIECES, 2 * BLOCK, DEPTH), half),
        pltpu.VMEM((low, LEVELS, slots, 2, BLOCK, BLOCK), half),
        pltpu.VMEM((low, slots, 2, BLOCK, BLOCK), half),
    ]
    vmem = max(57, sum(math.prod(a.shape) * 2 for a in buffers) // 1024**2 + 3) * 1024**2
    near, far = pl.pallas_call(
        functools.partial(kernel, nseg, ngrp),
        out_shape=(near, far),
        in_specs=[hbm] * 4,
        out_specs=(hbm, hbm),
        scratch_shapes=[pltpu.SMEM(a.shape, jnp.int32) for a in small]
        + buffers
        + [

            sems((2,)),
            sems((2, LEVELS, PIECES, PARTS)),
            sems((LEVELS, PIECES, PARTS)),
            sems((low, PIECES)),
            sems((low, PIECES)),
            sems((4, ngrp, PIECES)),
            sems((ngrp, PIECES)),
            sems((low, LEVELS)),
            sems((low,)),
            sems((nseg,)),
            sems((PIECES, PARTS)),
            sems((PIECES, PARTS)),
            sems((3,)),
            sems((nseg,)),
            sems,
            sems,
        ],
        compiler_params=pltpu.CompilerParams(
            collective_id=0, has_side_effects=True, vmem_limit_bytes=vmem
        ),
    )(*small, spectra)
    return (near, far[None, None])


def solution(mesh):
    placed = (
        P(None, None, None, ("seg", "grp")),
        P(),
        P("grp", None, None, None, None),
        P("grp", None, None),
    )
    return jax.shard_map(
        functools.partial(body, mesh.shape["seg"], mesh.shape["grp"]),
        mesh=mesh,
        in_specs=placed,
        out_specs=(
            P(None, None, ("seg", "grp"), None),
            P("seg", "grp", None, None, None, None, None),
        ),
        check_vma=False,
    )
```

```python
import functools
import math

import jax
import jax.numpy as jnp
from jax import lax
from jax.experimental import pallas as pl
from jax.experimental.pallas import tpu as pltpu
from jax.sharding import PartitionSpec as P

W = 8
F = 128
BAND_MAX = 48
SMOOTH = 4
BLOCK = 128
BLK_DEV = 3
DEPTH = W * 2 * BAND_MAX
PIECES = 2 * BLK_DEV
LEVELS = 4
PARTS = 2
CHUNK = 8
LIVE = (32, 40, 48)
CORES = 2


HIGH = lax.Precision.HIGHEST
MESH = pl.DeviceIdType.MESH


def whiten(m, depths, bins, spec, cols):
    power = jnp.zeros((F, BLOCK), jnp.float32)
    for w in range(W):
        for p in range(2):
            values = spec[m % 2, w, p].astype(jnp.float32)
            power = power + values * values
    f = lax.broadcasted_iota(jnp.int32, (F, F), 0)
    g = lax.broadcasted_iota(jnp.int32, (F, F), 1)
    window = jnp.where(jnp.abs(f - g) <= SMOOTH, 1.0, 0.0).astype(jnp.float32)
    totals = jnp.sum(window, axis=1, keepdims=True) * W
    level = jnp.dot(window, power, precision=HIGH, preferred_element_type=jnp.float32) / totals
    gain = lax.rsqrt(level + 1e-06)
    ahead = jnp.full((CHUNK, BLOCK), bins[0, 0], jnp.int32) == 0
    for p in range(2):
        for w in range(0, W, 2):
            low, high = [], []
            for v in (w, w + 1):
                low.append(spec[m % 2, v, p, :BAND_MAX].astype(jnp.float32) * gain[:BAND_MAX])
                high.append(
                    spec[m % 2, v, p, F - BAND_MAX :].astype(jnp.float32) * gain[F - BAND_MAX :]
                )
            for j in range(BAND_MAX // CHUNK):
                bin_of = slice(j * CHUNK, (j + 1) * CHUNK)
                first = ((j * 2 + p) * W + w) * CHUNK
                at = slice(first, first + 2 * CHUNK)
                for band in range(2):
                    if first < depths[band]:
                        pair = [
                            jnp.where(ahead == (band == 0), a[bin_of], b[bin_of])
                            for a, b in zip(low, high)
                        ]
                        cols[m * 2 + band, at] = jnp.concatenate(pair).astype(jnp.bfloat16)


class Gather:
    def __init__(self, axis, high, low, own, buf, send, recv):
        self.axis, self.high, self.low = axis, high, low
        self.own, self.buf, self.send, self.recv = own, buf, send, recv
        self.me = lax.axis_index(axis)
        self.p, self.l = lax.div(self.me, low), lax.rem(self.me, low)
        p, l = self.p, self.l
        self.dirs = [
            (p + 1 < high, self.me + low),
            (p > 0, self.me - low),
            (l + 1 < low, self.me + 1),
            (l > 0, self.me - 1),
        ]
        if high == 1:
            self.dirs[0] = self.dirs[1] = None
        if low == 1:
            self.dirs[2] = self.dirs[3] = None
        self.closing = False

    def greet(self, barrier):
        for entry in self.dirs:
            if entry is not None:

                @pl.when(entry[0])
                def _():
                    pl.semaphore_signal(
                        barrier, inc=1, device_id={self.axis: entry[1]}, device_id_type=MESH
                    )

    def peers(self):
        return sum(jnp.where(entry[0], 1, 0) for entry in self.dirs if entry is not None)

    def copy(self, way, src, q, own):
        return pltpu.make_async_remote_copy(
            src_ref=self.own.at[q, :self.depth] if own else self.buf.at[src, q, :self.depth],
            dst_ref=self.buf.at[src, q, :self.depth],
            send_sem=self.send.at[way, src, q],
            recv_sem=self.recv.at[src, q],
            device_id={self.axis: self.dirs[way][1]},
            device_id_type=MESH,
        )

    def pass_on(self, ways, src, q, own=False):
        for way in ways:
            if self.dirs[way] is not None:

                @pl.when(self.dirs[way][0])
                def _():
                    piece = self.copy(way, src, q, own)
                    if self.closing:
                        piece.wait_send()
                    else:
                        piece.start()

    def arrive(self, there, src, q, ways, use):
        @pl.when(there)
        def _():
            if not self.closing:
                piece = self.buf.at[src, q, :self.depth]
                pltpu.make_async_copy(piece, piece, self.recv.at[src, q]).wait()
            self.pass_on(ways, src, q)
            if use is not None and not self.closing:
                use(src, q)

    def start(self, q):
        self.pass_on((0, 1, 2, 3), self.me, q, own=True)

    def step(self, st, q, use, low_first=False):
        p, l, low = self.p, self.l, self.low
        turn = () if low_first else (2, 3)
        if 0 < st < self.high:
            self.arrive(p - st >= 0, (p - st) * low + l, q, (0,) + turn, use)
            self.arrive(p + st < self.high, (p + st) * low + l, q, (1,) + turn, use)
        d = st - 1
        if not 0 <= d < self.high:
            return
        for far, way in [(p, None)] if d == 0 else [(p - d, 0), (p + d, 1)]:
            inside = (far >= 0) & (far < self.high)
            for e in range(1, low):
                for there, other, on in ((l - e >= 0, l - e, 2), (l + e < low, l + e, 3)):
                    if not low_first:
                        ways = (on,)
                    elif d == 0:
                        ways = (0, 1, on)
                    else:
                        ways = (way,)
                    self.arrive(inside & there, far * low + other, q, ways, use)


def part_rows(depth, part):
    return pl.ds(part * (depth // PARTS), depth // PARTS)


class Line:
    def __init__(self, low, own, bufs, send, recv):
        self.low, self.own, self.bufs, self.send, self.recv = low, own, bufs, send, recv
        self.me = lax.axis_index("seg")
        self.z = lax.div(self.me, low)
        self.closing = False

    def slot(self, d, way):
        return d if d > 1 else 1 - way

    def buf(self, d, way):
        return self.bufs[self.slot(d, way)]

    def move(self, way, d, q, part):
        at = self.slot(d + 1, way)
        rows = part_rows(self.depth, part)
        piece = pltpu.make_async_remote_copy(
            src_ref=(self.buf(d, way) if d else self.own).at[q, rows],
            dst_ref=self.bufs[at].at[q, rows],
            send_sem=self.send.at[way, d, q, part],
            recv_sem=self.recv.at[at, q, part],
            device_id={"seg": self.me + (self.low if way else -self.low)},
            device_id_type=MESH,
        )
        if self.closing:
            piece.wait_send()
        else:
            piece.start()

    def start(self, q):
        z = self.z

        @pl.when((z + 1 < LEVELS) & (z != LEVELS - 2))
        def _():
            for part in range(PARTS):
                self.move(1, 0, q, part)

        @pl.when((z > 0) & (z != 1))
        def _():
            for part in range(PARTS):
                self.move(0, 0, q, part)

    def there(self, d):
        z = self.z
        left, right = z - d >= 0, z + d < LEVELS
        if d == 1:
            left, right = left & (z != LEVELS - 1), right & (z != 0)
        return ((left, z - d, z + 1 < LEVELS, 1), (right, z + d, z > 0, 0))

    def arrive(self, d, q, then=None):
        for part in range(PARTS):
            for here, _, on, way in self.there(d):

                @pl.when(here)
                def _():
                    if not self.closing:
                        at = self.slot(d, way)
                        piece = self.bufs[at].at[q, part_rows(self.depth, part)]
                        pltpu.make_async_copy(piece, piece, self.recv.at[at, q, part]).wait()

                    if d + 1 < LEVELS:

                        @pl.when(on)
                        def _():
                            self.move(way, d, q, part)

                    if then is not None:
                        then(q, part)


def kernel(
    nseg, ngrp, depths, bins_in, lists_in, counts_in, spectra, near_out, far_out,
    bins, lists, counts, near, far, spec, cols, left, right, two, three, side, grp_buf, ops, stage, end_stage,
    spec_sem, line_send, line_recv, side_send, side_recv, grp_send, grp_recv,
    far_send, end_send, far_recv, pass_send, pass_recv, small_sem, out_sem, move, near_sem,
):
    low = nseg // LEVELS
    slots = far.shape[1]
    line = Line(low, cols, (left, right, two, three), line_send, line_recv)
    grp = Gather("grp", ngrp // CORES, CORES, cols, grp_buf, grp_send, grp_recv)
    me, z = line.me, line.z
    y = lax.rem(me, low)
    mates = [lax.rem(y + e, low) for e in range(1, low)]
    before = lax.rem(y + low - 1, low)
    is_end = (z == 0) | (z == LEVELS - 1)
    inner = (z == 1) | (z == LEVELS - 2)
    end = jnp.where(z == 1, 0, LEVELS - 1)
    beside = jnp.where(z == 0, 1, LEVELS - 2)

    def load(m):
        return pltpu.make_async_copy(
            spectra.at[:, :, :, m * BLOCK : (m + 1) * BLOCK], spec.at[m % 2], spec_sem.at[m % 2]
        )

    small = [
        pltpu.make_async_copy(a, b, small_sem.at[k])
        for k, (a, b) in enumerate(((bins_in, bins), (lists_in, lists), (counts_in, counts)))
    ]
    for copy in small:
        copy.start()
    load(0).start()
    load(1).start()

    barrier = pltpu.get_barrier_semaphore()

    def greet(seg):
        pl.semaphore_signal(barrier, inc=1, device_id={"seg": seg}, device_id_type=MESH)

    for on, seg in ((z + 1 < LEVELS, me + low), (z > 0, me - low)):

        @pl.when(on)
        def _():
            greet(seg)

    for mate in mates:
        greet(z * low + mate)
    grp.greet(barrier)

    def side_copy(e, q):
        return pltpu.make_async_remote_copy(
            src_ref=cols.at[q, : line.depth],
            dst_ref=side.at[y, q, : line.depth],
            send_sem=side_send.at[e, q],
            recv_sem=side_recv.at[y, q],
            device_id={"seg": z * low + mates[e]},
            device_id_type=MESH,
        )

    def begin(q):
        line.start(q)
        for e in range(low - 1):
            if line.closing:
                side_copy(e, q).wait_send()
            else:
                side_copy(e, q).start()
        grp.start(q)

    def loop(fn, count):
        def step(q, carry):
            fn(q)
            return carry

        lax.fori_loop(0, count, step, 0)

    def one(fn, m, band):
        line.depth = grp.depth = depths[band]
        fn(2 * m + band)

    def each(fn):
        def step(m):
            for band in range(2):
                one(fn, m, band)

        loop(step, BLK_DEV)

    for copy in small:
        copy.wait()
    for m in range(BLK_DEV):
        load(m).wait()
        whiten(m, depths, bins, spec, cols)
        if m + 2 < BLK_DEV:
            load(m + 2).start()
        if m == 0:
            inner_peers = jnp.where(z + 1 < LEVELS, 1, 0) + jnp.where(z > 0, 1, 0)
            pl.semaphore_wait(barrier, inner_peers + (low - 1) + grp.peers())
        one(begin, m, 0)
        one(begin, m, 1)

    if depths[1] < DEPTH:
        rest = jnp.zeros((DEPTH - depths[1], BLOCK), jnp.bfloat16)
        for m in range(BLK_DEV):
            for buf in [cols, left, right, two, three] + [side.at[mate] for mate in mates]:
                buf[2 * m + 1, depths[1] :] = rest

    own = pltpu.make_async_copy(cols, side.at[y], move)
    own.start()

    def operands(slot, q, piece):
        band = lax.rem(q, 2)
        lane = lax.broadcasted_iota(jnp.int32, (1, BLOCK), 1)
        sign = jnp.where(lane < BLOCK // 2, 1.0, -1.0).astype(jnp.float32)
        for j in range(DEPTH // BLOCK):
            at = slice(j * BLOCK, (j + 1) * BLOCK)
            live = jnp.where(j * CHUNK + lax.rem(lane, CHUNK) < bins[band, 1], 1.0, 0.0)
            rows = jnp.transpose(piece[at].astype(jnp.float32)) * live.astype(jnp.float32)
            ops[slot, q, :BLOCK, at] = rows.astype(jnp.bfloat16)
            twisted = pltpu.roll(rows, BLOCK // 2, 1) * sign
            ops[slot, q, BLOCK:, at] = twisted.astype(jnp.bfloat16)

    each(lambda q: operands(y, q, cols[q]))

    def scale(band):
        return lax.rsqrt(jnp.full((1, BLOCK), W * bins[band, 1], jnp.int32).astype(jnp.float32))

    def near_from(piece, src, q):
        m, band = lax.div(q, 2), lax.rem(q, 2)
        at = pl.ds(pl.multiple_of(src * (BLK_DEV * BLOCK) + m * BLOCK, BLOCK), BLOCK)
        for i in range(BLK_DEV):
            rows = ops[y, i * 2 + band, :, : line.depth]
            prod = jnp.dot(rows, piece, preferred_element_type=jnp.float32)
            prod = (prod * scale(band)).astype(jnp.bfloat16)
            near[band, 0, i * BLOCK : (i + 1) * BLOCK, at] = prod[:BLOCK]
            near[band, 1, i * BLOCK : (i + 1) * BLOCK, at] = prod[BLOCK:]

    def use_near(src, q):
        near_from(grp_buf[src, q, : line.depth], src, q)

    each(lambda q: near_from(cols[q, : line.depth], grp.me, q))

    def pair(owner, slot, src, t, dst, c):
        i, m, band = lists[owner, 0, c, t], lists[owner, 1, c, t], lists[owner, 2, c, t]
        factor = jnp.where(c < counts[owner, t], scale(band), 0.0)
        prod = jnp.dot(
            ops[slot, i * 2 + band], src[m * 2 + band], preferred_element_type=jnp.float32
        )
        prod = (prod * factor).astype(jnp.bfloat16)
        dst[c, 0] = prod[:BLOCK]
        dst[c, 1] = prod[BLOCK:]

    def pass_on(q, part):
        rows = part_rows(line.depth, part)
        piece = pltpu.make_async_remote_copy(
            src_ref=three.at[q, rows],
            dst_ref=left.at[q, rows],
            send_sem=pass_send.at[q, part],
            recv_sem=pass_recv.at[q, part],
            device_id={"seg": z * low + mates[0]},
            device_id_type=MESH,
        )
        if line.closing:
            piece.wait_send()
        else:
            piece.start()

    def passed(q):
        for part in range(PARTS):
            piece = left.at[q, part_rows(line.depth, part)]
            pltpu.make_async_copy(piece, piece, pass_recv.at[q, part]).wait()

    def level_pairs(buf, src, c, others):
        t = src * low + y
        pair(me, y, buf, t, far.at[t], c)
        for mate in others:
            pair(z * low + mate, mate, buf, t, stage.at[mate, src], c)

    def hand_over(src, others):
        for mate in others:
            piece = pltpu.make_async_remote_copy(
                src_ref=stage.at[mate, src],
                dst_ref=far.at[src * low + y],
                send_sem=far_send.at[mate, src],
                recv_sem=far_recv.at[src * low + y],
                device_id={"seg": z * low + mate},
                device_id_type=MESH,
            )
            if line.closing:
                piece.wait_send()
            else:
                piece.start()

    def end_copy(other):
        return pltpu.make_async_remote_copy(
            src_ref=end_stage.at[other],
            dst_ref=far.at[z * low + other],
            send_sem=end_send.at[other],
            recv_sem=far_recv.at[z * low + other],
            device_id={"seg": end * low + y},
            device_id_type=MESH,
        )

    def for_end():
        for at, buf in ((1, left), (LEVELS - 2, right)):

            @pl.when(z == at)
            def _():
                each(lambda q: operands(low, q, buf[q]))

        @pl.when(inner)
        def _():
            for other in [y] + mates:
                t = z * low + other
                loop(
                    lambda c: pair(end * low + y, low, side.at[other], t, end_stage.at[other], c),
                    slots,
                )
                end_copy(other).start()

    def first(q):
        line.arrive(1, q)
        grp.step(1, q, None if grp.closing else use_near)
        if not line.closing:
            for mate in mates:
                piece = side.at[mate, q, : line.depth]
                pltpu.make_async_copy(piece, piece, side_recv.at[mate, q]).wait()
                operands(mate, q, side[mate, q])

    def second(q):
        line.arrive(2, q)
        grp.step(2, q, None if grp.closing else use_near)
        if not line.closing:

            @pl.when(q < slots)
            def _():
                for mate in mates:
                    t = z * low + mate
                    pair(me, y, side.at[mate], t, far.at[t], q)
                for here, src, _, way in line.there(1):

                    @pl.when(here)
                    def _():
                        level_pairs(line.buf(1, way), src, q, mates)

                        @pl.when(q == slots - 1)
                        def _():
                            hand_over(src, mates)

    def later(d):
        def step(q):
            if d < LEVELS:
                line.arrive(d, q, pass_on if d == LEVELS - 1 else None)
            grp.step(d, q, None if grp.closing else use_near)

        each(step)

    def after(d):
        last = d == LEVELS - 1
        others = mates[1:] if last else mates
        for here, src, _, way in line.there(d):

            @pl.when(here)
            def _():
                if not line.closing:
                    loop(lambda c: level_pairs(line.buf(d, way), src, c, others), slots)
                hand_over(src, others)
                if last and not line.closing:
                    each(passed)
                    t = src * low + before
                    loop(lambda c: pair(me, y, left, t, far.at[t], c), slots)

    each(first)
    own.wait()
    far[me] = jnp.zeros(far.shape[1:], far.dtype)
    for_end()
    each(second)
    near_copy = pltpu.make_async_copy(near, near_out, near_sem)
    if grp.high < 3:
        near_copy.start()
    after(2)
    for d in range(3, max(LEVELS, grp.high + 1)):
        later(d)
        if d == grp.high:
            near_copy.start()
        if d < LEVELS:
            after(d)

    line.closing = grp.closing = True
    each(begin)
    each(first)
    after(1)
    each(second)
    after(2)
    for d in range(3, max(LEVELS, grp.high + 1)):
        later(d)
        if d < LEVELS:
            after(d)

    @pl.when(inner)
    def _():
        for other in [y] + mates:
            end_copy(other).wait_send()

    def far_copy(t):
        return pltpu.make_async_copy(far.at[t], far_out.at[t], out_sem.at[t])

    def landed(t):
        tz, ty = lax.div(t, low), lax.rem(t, low)

        handed = (ty != y) & (tz != z) & ~(is_end & (tz == LEVELS - 1 - z) & (ty == before))

        @pl.when(handed | (is_end & (tz == beside) & (ty == y)))
        def _():
            pltpu.make_async_copy(far.at[t], far.at[t], far_recv.at[t]).wait()

        far_copy(t).start()

    loop(landed, nseg)
    loop(lambda t: far_copy(t).wait(), nseg)
    near_copy.wait()


def call(nseg, ngrp, which, spectra, band_bins, far_list, far_count):
    depths = (DEPTH, 2 * W * LIVE[which])
    slots = far_list.shape[3]
    low = nseg // LEVELS
    hbm = pl.BlockSpec(memory_space=pl.ANY)
    sems = pltpu.SemaphoreType.DMA
    half = jnp.bfloat16
    small = (band_bins, jnp.transpose(far_list[0], (0, 3, 2, 1)), far_count[0])
    near = jax.ShapeDtypeStruct((2, 2, BLK_DEV * BLOCK, ngrp * BLK_DEV * BLOCK), half)
    far = jax.ShapeDtypeStruct((nseg, slots, 2, BLOCK, BLOCK), half)
    buffers = [
        pltpu.VMEM(near.shape, half),
        pltpu.VMEM(far.shape, half),
        pltpu.VMEM((2, W, 2, F, BLOCK), half),
        pltpu.VMEM((PIECES, DEPTH, BLOCK), half),
        pltpu.VMEM((PIECES, DEPTH, BLOCK), half),
        pltpu.VMEM((PIECES, DEPTH, BLOCK), half),
        pltpu.VMEM((PIECES, DEPTH, BLOCK), half),
        pltpu.VMEM((PIECES, DEPTH, BLOCK), half),
        pltpu.VMEM((low, PIECES, DEPTH, BLOCK), half),
        pltpu.VMEM((ngrp, PIECES, DEPTH, BLOCK), half),
        pltpu.VMEM((low + 1, PIECES, 2 * BLOCK, DEPTH), half),
        pltpu.VMEM((low, LEVELS, slots, 2, BLOCK, BLOCK), half),
        pltpu.VMEM((low, slots, 2, BLOCK, BLOCK), half),
    ]
    vmem = max(57, sum(math.prod(a.shape) * 2 for a in buffers) // 1024**2 + 3) * 1024**2
    near, far = pl.pallas_call(
        functools.partial(kernel, nseg, ngrp, depths),
        out_shape=(near, far),
        in_specs=[hbm] * 4,
        out_specs=(hbm, hbm),
        scratch_shapes=[pltpu.SMEM(a.shape, jnp.int32) for a in small]
        + buffers
        + [

            sems((2,)),
            sems((2, LEVELS, PIECES, PARTS)),
            sems((LEVELS, PIECES, PARTS)),
            sems((low, PIECES)),
            sems((low, PIECES)),
            sems((4, ngrp, PIECES)),
            sems((ngrp, PIECES)),
            sems((low, LEVELS)),
            sems((low,)),
            sems((nseg,)),
            sems((PIECES, PARTS)),
            sems((PIECES, PARTS)),
            sems((3,)),
            sems((nseg,)),
            sems,
            sems,
        ],
        compiler_params=pltpu.CompilerParams(
            collective_id=which, has_side_effects=True, vmem_limit_bytes=vmem
        ),
    )(*small, spectra)
    return (near, far[None, None])


def body(nseg, ngrp, *args):
    count = args[1][1, 1]
    which = sum((count > live).astype(jnp.int32) for live in LIVE[:-1])
    calls = [functools.partial(call, nseg, ngrp, k) for k in range(len(LIVE))]
    return lax.switch(which, calls, *args)


def solution(mesh):
    placed = (
        P(None, None, None, ("seg", "grp")),
        P(),
        P("grp", None, None, None, None),
        P("grp", None, None),
    )
    return jax.shard_map(
        functools.partial(body, mesh.shape["seg"], mesh.shape["grp"]),
        mesh=mesh,
        in_specs=placed,
        out_specs=(
            P(None, None, ("seg", "grp"), None),
            P("seg", "grp", None, None, None, None, None),
        ),
        check_vma=False,
    )
```

```python
import functools
import math

import jax
import jax.numpy as jnp
from jax import lax
from jax.experimental import pallas as pl
from jax.experimental.pallas import tpu as pltpu
from jax.sharding import PartitionSpec as P

W = 8
F = 128
BAND_MAX = 48
SMOOTH = 4
BLOCK = 128
BLK_DEV = 3
DEPTH = W * 2 * BAND_MAX
PIECES = 2 * BLK_DEV
LEVELS = 4
PARTS = 2
LIMIT = 62 * 1024**2
CORES = 2


HIGH = lax.Precision.HIGHEST
MESH = pl.DeviceIdType.MESH


def whiten(m, small, spec, cols):
    power = jnp.zeros((F, BLOCK), jnp.float32)
    for w in range(W):
        for p in range(2):
            values = spec[w, p, :, m * BLOCK : (m + 1) * BLOCK].astype(jnp.float32)
            power = power + values * values
    f = lax.broadcasted_iota(jnp.int32, (F, F), 0)
    g = lax.broadcasted_iota(jnp.int32, (F, F), 1)
    window = jnp.where(jnp.abs(f - g) <= SMOOTH, 1.0, 0.0).astype(jnp.float32)
    totals = jnp.sum(window, axis=1, keepdims=True) * W
    level = jnp.dot(window, power, precision=HIGH, preferred_element_type=jnp.float32) / totals
    gain = lax.rsqrt(level + 1e-06)
    here = slice(m * BLOCK, (m + 1) * BLOCK)
    ahead = jnp.full((BAND_MAX, BLOCK), small[0, 4, 0, 0], jnp.int32) == 0
    for p in range(2):
        for w in range(W):
            at = slice((p * W + w) * BAND_MAX, (p * W + w + 1) * BAND_MAX)
            low = spec[w, p, :BAND_MAX, here].astype(jnp.float32) * gain[:BAND_MAX]
            high = spec[w, p, F - BAND_MAX :, here].astype(jnp.float32) * gain[F - BAND_MAX :]
            cols[m * 2, at] = jnp.where(ahead, low, high).astype(jnp.bfloat16)
            cols[m * 2 + 1, at] = jnp.where(ahead, high, low).astype(jnp.bfloat16)


class Gather:
    def __init__(self, axis, high, low, own, buf, send, recv):
        self.axis, self.high, self.low = axis, high, low
        self.own, self.buf, self.send, self.recv = own, buf, send, recv
        self.me = lax.axis_index(axis)
        self.p, self.l = lax.div(self.me, low), lax.rem(self.me, low)
        p, l = self.p, self.l
        self.dirs = [
            (p + 1 < high, self.me + low),
            (p > 0, self.me - low),
            (l + 1 < low, self.me + 1),
            (l > 0, self.me - 1),
        ]
        if high == 1:
            self.dirs[0] = self.dirs[1] = None
        if low == 1:
            self.dirs[2] = self.dirs[3] = None
        self.closing = False

    def greet(self, barrier):
        for entry in self.dirs:
            if entry is not None:

                @pl.when(entry[0])
                def _():
                    pl.semaphore_signal(
                        barrier, inc=1, device_id={self.axis: entry[1]}, device_id_type=MESH
                    )

    def peers(self):
        return sum(jnp.where(entry[0], 1, 0) for entry in self.dirs if entry is not None)

    def copy(self, way, src, q, own):
        return pltpu.make_async_remote_copy(
            src_ref=self.own.at[q] if own else self.buf.at[src, q],
            dst_ref=self.buf.at[src, q],
            send_sem=self.send.at[way, src, q],
            recv_sem=self.recv.at[src, q],
            device_id={self.axis: self.dirs[way][1]},
            device_id_type=MESH,
        )

    def pass_on(self, ways, src, q, own=False):
        for way in ways:
            if self.dirs[way] is not None:

                @pl.when(self.dirs[way][0])
                def _():
                    piece = self.copy(way, src, q, own)
                    if self.closing:
                        piece.wait_send()
                    else:
                        piece.start()

    def arrive(self, there, src, q, ways, use):
        @pl.when(there)
        def _():
            if not self.closing:
                pltpu.make_async_copy(
                    self.buf.at[src, q], self.buf.at[src, q], self.recv.at[src, q]
                ).wait()
            self.pass_on(ways, src, q)
            if use is not None and not self.closing:
                use(src, q)

    def start(self, q):
        self.pass_on((0, 1, 2, 3), self.me, q, own=True)

    def step(self, st, q, use, low_first=False):
        p, l, low = self.p, self.l, self.low
        turn = () if low_first else (2, 3)
        if 0 < st < self.high:
            self.arrive(p - st >= 0, (p - st) * low + l, q, (0,) + turn, use)
            self.arrive(p + st < self.high, (p + st) * low + l, q, (1,) + turn, use)
        d = st - 1
        if not 0 <= d < self.high:
            return
        for far, way in [(p, None)] if d == 0 else [(p - d, 0), (p + d, 1)]:
            inside = (far >= 0) & (far < self.high)
            for e in range(1, low):
                for there, other, on in ((l - e >= 0, l - e, 2), (l + e < low, l + e, 3)):
                    if not low_first:
                        ways = (on,)
                    elif d == 0:
                        ways = (0, 1, on)
                    else:
                        ways = (way,)
                    self.arrive(inside & there, far * low + other, q, ways, use)


def part_rows(part):
    return pl.ds(part * (DEPTH // PARTS), DEPTH // PARTS)


class Line:
    def __init__(self, low, own, bufs, send, recv):
        self.low, self.own, self.bufs, self.send, self.recv = low, own, bufs, send, recv
        self.me = lax.axis_index("seg")
        self.z = lax.div(self.me, low)
        self.late = lax.rem(lax.axis_index("grp"), CORES) == CORES - 1
        self.turns = low == 2 and CORES == 2
        self.closing = False

    def slot(self, d, way):
        return d if d > 1 else 1 - way

    def buf(self, d, way):
        return self.bufs[self.slot(d, way)]

    def move(self, way, d, q, part):
        at = self.slot(d + 1, way)
        rows = part_rows(part)
        piece = pltpu.make_async_remote_copy(
            src_ref=(self.buf(d, way) if d else self.own).at[q, rows],
            dst_ref=self.bufs[at].at[q, rows],
            send_sem=self.send.at[way, d, q, part],
            recv_sem=self.recv.at[at, q, part],
            device_id={"seg": self.me + (self.low if way else -self.low)},
            device_id_type=MESH,
        )
        if self.closing:
            piece.wait_send()
        else:
            piece.start()

    def start(self, q):
        z = self.z

        @pl.when((z + 1 < LEVELS) & (z != LEVELS - 2))
        def _():
            for part in range(PARTS):
                self.move(1, 0, q, part)

        @pl.when((z > 0) & (z != 1))
        def _():
            for part in range(PARTS):
                self.move(0, 0, q, part)

    def there(self, d):
        z = self.z
        left, right = z - d >= 0, z + d < LEVELS
        on_right, on_left = z + 1 < LEVELS, z > 0
        if d == 1:
            left, right = left & (z != LEVELS - 1), right & (z != 0)
        if self.turns and d == 1:
            first = jnp.logical_not(self.late) & (not self.closing)
            on_right, on_left = on_right & (first | (z != 1)), on_left & (first | (z != LEVELS - 2))
        elif self.turns and d == 2:
            on_right, on_left = on_right & self.late, on_left & self.late
        elif self.turns:
            left, right = left & self.late, right & self.late
        return ((left, z - d, on_right, 1), (right, z + d, on_left, 0))

    def cross(self, q):
        for at, way in ((1, 1), (LEVELS - 2, 0)):

            @pl.when(self.z == at)
            def _():
                for part in range(PARTS):
                    self.move(way, 1, q, part)

    def arrive(self, d, q, then=None):
        for part in range(PARTS):
            for here, _, on, way in self.there(d):

                @pl.when(here)
                def _():
                    if not self.closing:
                        at = self.slot(d, way)
                        piece = self.bufs[at].at[q, part_rows(part)]
                        pltpu.make_async_copy(piece, piece, self.recv.at[at, q, part]).wait()

                    if d + 1 < LEVELS:

                        @pl.when(on)
                        def _():
                            self.move(way, d, q, part)

                    if then is not None:
                        then(q, part)


def kernel(
    nseg, ngrp, small, spec, near, far, cols, left, right, two, three, side, grp_buf, ops, stage, end_stage,
    line_send, line_recv, side_send, side_recv, grp_send, grp_recv,
    far_send, end_send, far_recv, pass_send, pass_recv,
    turn_stage, turn_send, rows_send, rows_recv, go, move,
):
    low = nseg // LEVELS
    slots = far.shape[1]
    line = Line(low, cols, (left, right, two, three), line_send, line_recv)
    grp = Gather("grp", ngrp // CORES, CORES, cols, grp_buf, grp_send, grp_recv)
    me, z = line.me, line.z
    y = lax.rem(me, low)
    mates = [lax.rem(y + e, low) for e in range(1, low)]
    before = lax.rem(y + low - 1, low)
    is_end = (z == 0) | (z == LEVELS - 1)
    inner = (z == 1) | (z == LEVELS - 2)
    end = jnp.where(z == 1, 0, LEVELS - 1)
    beside = jnp.where(z == 0, 1, LEVELS - 2)

    barrier = pltpu.get_barrier_semaphore()

    def greet(seg):
        pl.semaphore_signal(barrier, inc=1, device_id={"seg": seg}, device_id_type=MESH)

    for on, seg in ((z + 1 < LEVELS, me + low), (z > 0, me - low)):

        @pl.when(on)
        def _():
            greet(seg)

    for mate in mates:
        greet(z * low + mate)
        if line.turns:

            @pl.when(is_end)
            def _():
                greet(beside * low + mate)

    late = line.late
    early = jnp.logical_not(late)
    grp.greet(barrier)

    def side_copy(e, q):
        return pltpu.make_async_remote_copy(
            src_ref=cols.at[q],
            dst_ref=side.at[y, q],
            send_sem=side_send.at[e, q],
            recv_sem=side_recv.at[y, q],
            device_id={"seg": z * low + mates[e]},
            device_id_type=MESH,
        )

    def begin(q):
        line.start(q)
        for e in range(low - 1):
            if line.closing:
                side_copy(e, q).wait_send()
            else:
                side_copy(e, q).start()
        grp.start(q)

    def loop(fn, count=PIECES):
        def step(q, carry):
            fn(q)
            return carry

        lax.fori_loop(0, count, step, 0)

    for m in range(BLK_DEV):
        whiten(m, small, spec, cols)
        if m == 0:
            inner_peers = jnp.where(z + 1 < LEVELS, 1, 0) + jnp.where(z > 0, 1, 0)
            if line.turns:
                inner_peers += jnp.where(inner, low - 1, 0)
            pl.semaphore_wait(barrier, inner_peers + (low - 1) + grp.peers())
        begin(2 * m)
        begin(2 * m + 1)

    own = pltpu.make_async_copy(cols, side.at[y], move)
    own.start()

    half = DEPTH // 2

    def operands(slot, q, piece):
        band = lax.rem(q, 2)
        bin_of = lax.rem(lax.broadcasted_iota(jnp.int32, (1, DEPTH), 1), BAND_MAX)
        live = jnp.where(bin_of < small[band, 4, 1, 0], 1.0, 0.0).astype(jnp.float32)
        rows = jnp.transpose(piece.astype(jnp.float32)) * live
        ops[slot, q, :BLOCK] = rows.astype(jnp.bfloat16)
        ops[slot, q, BLOCK:, :half] = rows[:, half:].astype(jnp.bfloat16)
        ops[slot, q, BLOCK:, half:] = (-rows[:, :half]).astype(jnp.bfloat16)

    loop(lambda q: operands(y, q, cols[q]))

    def scale(band):
        return lax.rsqrt(jnp.full((1, BLOCK), W * small[band, 4, 1, 0], jnp.int32).astype(jnp.float32))

    def near_from(piece, src, q):
        m, band = lax.div(q, 2), lax.rem(q, 2)
        at = pl.ds(pl.multiple_of(src * (BLK_DEV * BLOCK) + m * BLOCK, BLOCK), BLOCK)
        for i in range(BLK_DEV):
            prod = jnp.dot(ops[y, i * 2 + band], piece, preferred_element_type=jnp.float32)
            prod = (prod * scale(band)).astype(jnp.bfloat16)
            near[band, 0, i * BLOCK : (i + 1) * BLOCK, at] = prod[:BLOCK]
            near[band, 1, i * BLOCK : (i + 1) * BLOCK, at] = prod[BLOCK:]

    def use_near(src, q):
        near_from(grp_buf[src, q], src, q)

    loop(lambda q: near_from(cols[q], grp.me, q))

    def pair(owner, slot, src, t, dst, c):
        i, m, band = small[owner, 0, c, t], small[owner, 1, c, t], small[owner, 2, c, t]
        factor = jnp.where(c < small[owner, 3, 0, t], scale(band), 0.0)
        prod = jnp.dot(
            ops[slot, i * 2 + band], src[m * 2 + band], preferred_element_type=jnp.float32
        )
        prod = (prod * factor).astype(jnp.bfloat16)
        dst[c, 0] = prod[:BLOCK]
        dst[c, 1] = prod[BLOCK:]

    def pass_on(q, part):
        rows = part_rows(part)
        piece = pltpu.make_async_remote_copy(
            src_ref=three.at[q, rows],
            dst_ref=left.at[q, rows],
            send_sem=pass_send.at[q, part],
            recv_sem=pass_recv.at[q, part],
            device_id={"seg": z * low + mates[0]},
            device_id_type=MESH,
        )
        if line.closing:
            piece.wait_send()
        else:
            piece.start()

    def passed(q):
        for part in range(PARTS):
            piece = left.at[q, part_rows(part)]
            pltpu.make_async_copy(piece, piece, pass_recv.at[q, part]).wait()

    def level_pairs(buf, src, c, others):
        t = src * low + y
        pair(me, y, buf, t, far.at[t], c)
        for mate in others:
            pair(z * low + mate, mate, buf, t, stage.at[mate, src], c)

    def hand_over(src, others):
        for mate in others:
            piece = pltpu.make_async_remote_copy(
                src_ref=stage.at[mate, src],
                dst_ref=far.at[src * low + y],
                send_sem=far_send.at[mate, src],
                recv_sem=far_recv.at[src * low + y],
                device_id={"seg": z * low + mate},
                device_id_type=MESH,
            )
            if line.closing:
                piece.wait_send()
            else:
                piece.start()

    def end_copy(other):
        return pltpu.make_async_remote_copy(
            src_ref=end_stage.at[other],
            dst_ref=far.at[z * low + other],
            send_sem=end_send.at[other],
            recv_sem=far_recv.at[z * low + other],
            device_id={"seg": end * low + y},
            device_id_type=MESH,
        )

    def for_end():
        for at, buf in ((1, left), (LEVELS - 2, right)):

            @pl.when(z == at)
            def _():
                loop(lambda q: operands(low, q, buf[q]))

        @pl.when(inner)
        def _():
            for other in [y] + mates:
                t = z * low + other
                loop(
                    lambda c: pair(end * low + y, low, side.at[other], t, end_stage.at[other], c),
                    slots,
                )
                end_copy(other).start()

    def rows_copy(q):
        return pltpu.make_async_remote_copy(
            src_ref=side.at[mates[0], q],
            dst_ref=three.at[q],
            send_sem=rows_send.at[q],
            recv_sem=rows_recv.at[q],
            device_id={"seg": beside * low + y},
            device_id_type=MESH,
        )

    def turn_copy(k):
        t = (LEVELS - 1 - end) * low + y
        return pltpu.make_async_remote_copy(
            src_ref=turn_stage.at[k],
            dst_ref=far.at[t],
            send_sem=turn_send.at[k],
            recv_sem=far_recv.at[t],
            device_id={"seg": end * low + (mates[0] if k else y)},
            device_id_type=MESH,
        )

    def turn_pairs():
        t = (LEVELS - 1 - end) * low + y
        for k, owner in enumerate((y, mates[0])):
            loop(
                lambda c: pair(end * low + owner, low + k, two, t, turn_stage.at[k], c), slots
            )
            turn_copy(k).start()

    def first(q):
        line.arrive(1, q)
        grp.step(1, q, None if grp.closing else use_near)
        if not line.closing:
            for mate in mates:
                pltpu.make_async_copy(
                    side.at[mate, q], side.at[mate, q], side_recv.at[mate, q]
                ).wait()
                operands(mate, q, side[mate, q])
        if line.turns:

            @pl.when(is_end & early)
            def _():
                if line.closing:
                    rows_copy(q).wait_send()
                else:
                    rows_copy(q).start()

    def second(q):
        line.arrive(2, q)
        grp.step(2, q, None if grp.closing else use_near)
        if line.turns and not line.closing:

            @pl.when(inner & early)
            def _():
                pltpu.make_async_copy(three.at[q], three.at[q], rows_recv.at[q]).wait()
                operands(low + 1, q, three[q])

        if not line.closing:

            @pl.when(q < slots)
            def _():
                for mate in mates:
                    t = z * low + mate
                    pair(me, y, side.at[mate], t, far.at[t], q)
                for here, src, _, way in line.there(1):

                    @pl.when(here)
                    def _():
                        level_pairs(line.buf(1, way), src, q, mates)

                        @pl.when(q == slots - 1)
                        def _():
                            hand_over(src, mates)

    def later(d):
        def step(q):
            if d < LEVELS:
                line.arrive(d, q, pass_on if d == LEVELS - 1 else None)
            grp.step(d, q, None if grp.closing else use_near)

        loop(step)

    def after(d):
        last = d == LEVELS - 1
        others = mates[1:] if last else mates
        for here, src, _, way in line.there(d):

            @pl.when(here)
            def _():
                if not line.closing:
                    loop(lambda c: level_pairs(line.buf(d, way), src, c, others), slots)
                hand_over(src, others)
                if last and not line.closing:
                    loop(passed)
                    t = src * low + before
                    loop(lambda c: pair(me, y, left, t, far.at[t], c), slots)

    loop(first)
    own.wait()
    far[me] = jnp.zeros(far.shape[1:], far.dtype)
    for_end()
    if line.turns:

        @pl.when(inner & late)
        def _():
            pl.semaphore_wait(go, 1)
            loop(line.cross)

    loop(second)
    if line.turns:

        @pl.when(inner & early)
        def _():
            line.closing = True
            loop(line.cross)
            line.closing = False
            pl.semaphore_signal(
                go, inc=1, device_id={"grp": grp.me + 1}, device_id_type=MESH
            )
            turn_pairs()

    after(2)
    for d in range(3, max(LEVELS, grp.high + 1)):
        later(d)
        if d < LEVELS:
            after(d)

    line.closing = grp.closing = True
    loop(begin)
    loop(first)
    after(1)
    loop(second)
    after(2)
    for d in range(3, max(LEVELS, grp.high + 1)):
        later(d)
        if d < LEVELS:
            after(d)

    @pl.when(inner)
    def _():
        for other in [y] + mates:
            end_copy(other).wait_send()

    if line.turns:

        @pl.when(inner & late)
        def _():
            loop(line.cross)

        @pl.when(inner & early)
        def _():
            for k in range(2):
                turn_copy(k).wait_send()

    def landed(t):
        tz, ty = lax.div(t, low), lax.rem(t, low)

        across = is_end & (tz == LEVELS - 1 - z)
        passed_on = across & (ty == before)
        handed = is_end & (tz == beside) & (ty == y)
        if line.turns:
            passed_on, handed = passed_on & late, handed | (across & (ty == y) & early)

        @pl.when(handed | ((ty != y) & (tz != z) & jnp.logical_not(passed_on)))
        def _():
            pltpu.make_async_copy(far.at[t], far.at[t], far_recv.at[t]).wait()

    loop(landed, nseg)


def body(nseg, ngrp, spectra, band_bins, far_list, far_count):
    slots = far_list.shape[3]
    low = nseg // LEVELS
    smem = pl.BlockSpec(memory_space=pltpu.SMEM)
    whole = pl.BlockSpec(memory_space=pltpu.VMEM)
    sems = pltpu.SemaphoreType.DMA
    half = jnp.bfloat16
    shape = (nseg, 1, slots, nseg)
    small = jnp.concatenate(
        [
            jnp.transpose(far_list[0], (0, 3, 2, 1)),
            jnp.broadcast_to(far_count[0][:, None, None], shape),
            jnp.pad(band_bins[:, None, :, None], [(0, n - k) for n, k in zip(shape, (2, 1, 2, 1))]),
        ],
        axis=1,
    )
    near = jax.ShapeDtypeStruct((2, 2, BLK_DEV * BLOCK, ngrp * BLK_DEV * BLOCK), half)
    far = jax.ShapeDtypeStruct((nseg, slots, 2, BLOCK, BLOCK), half)
    buffers = [
        pltpu.VMEM((PIECES, DEPTH, BLOCK), half),
        pltpu.VMEM((PIECES, DEPTH, BLOCK), half),
        pltpu.VMEM((PIECES, DEPTH, BLOCK), half),
        pltpu.VMEM((PIECES, DEPTH, BLOCK), half),
        pltpu.VMEM((PIECES, DEPTH, BLOCK), half),
        pltpu.VMEM((low, PIECES, DEPTH, BLOCK), half),
        pltpu.VMEM((ngrp, PIECES, DEPTH, BLOCK), half),
        pltpu.VMEM((low + (2 if low == 2 else 1), PIECES, 2 * BLOCK, DEPTH), half),
        pltpu.VMEM((low, LEVELS, slots, 2, BLOCK, BLOCK), half),
        pltpu.VMEM((low, slots, 2, BLOCK, BLOCK), half),
    ]
    kept = sum(math.prod(a.shape) * 2 for a in buffers + [near, far, spectra])
    vmem = min(kept + 2 * 1024**2, LIMIT)
    near, far = pl.pallas_call(
        functools.partial(kernel, nseg, ngrp),
        out_shape=(near, far),
        in_specs=[smem, whole],
        out_specs=(whole, whole),
        scratch_shapes=buffers
        + [

            sems((2, LEVELS, PIECES, PARTS)),
            sems((LEVELS, PIECES, PARTS)),
            sems((low, PIECES)),
            sems((low, PIECES)),
            sems((4, ngrp, PIECES)),
            sems((ngrp, PIECES)),
            sems((low, LEVELS)),
            sems((low,)),
            sems((nseg,)),
            sems((PIECES, PARTS)),
            sems((PIECES, PARTS)),
            pltpu.VMEM((2, slots, 2, BLOCK, BLOCK), half),
            sems((2,)),
            sems((PIECES,)),
            sems((PIECES,)),
            pltpu.SemaphoreType.REGULAR,
            sems,
        ],
        compiler_params=pltpu.CompilerParams(
            collective_id=0, has_side_effects=True, vmem_limit_bytes=vmem
        ),
    )(small, spectra)
    return (near, far[None, None])


def solution(mesh):
    placed = (
        P(None, None, None, ("seg", "grp")),
        P(),
        P("grp", None, None, None, None),
        P("grp", None, None),
    )
    return jax.shard_map(
        functools.partial(body, mesh.shape["seg"], mesh.shape["grp"]),
        mesh=mesh,
        in_specs=placed,
        out_specs=(
            P(None, None, ("seg", "grp"), None),
            P("seg", "grp", None, None, None, None, None),
        ),
        check_vma=False,
    )
```

```python
import functools
import math

import jax
import jax.numpy as jnp
from jax import lax
from jax.experimental import pallas as pl
from jax.experimental.pallas import tpu as pltpu
from jax.sharding import PartitionSpec as P

W = 8
F = 128
BAND_MAX = 48
SMOOTH = 4
BLOCK = 128
BLK_DEV = 3
DEPTH = W * 2 * BAND_MAX
PIECES = 2 * BLK_DEV
LEVELS = 4
PARTS = 2
LIMIT = 62 * 1024**2
CORES = 2


HIGH = lax.Precision.HIGHEST
MESH = pl.DeviceIdType.MESH


def whiten(m, small, spec, cols):
    power = jnp.zeros((F, BLOCK), jnp.float32)
    for w in range(W):
        for p in range(2):
            values = spec[w, p, :, m * BLOCK : (m + 1) * BLOCK].astype(jnp.float32)
            power = power + values * values
    f = lax.broadcasted_iota(jnp.int32, (F, F), 0)
    g = lax.broadcasted_iota(jnp.int32, (F, F), 1)
    window = jnp.where(jnp.abs(f - g) <= SMOOTH, 1.0, 0.0).astype(jnp.float32)
    totals = jnp.sum(window, axis=1, keepdims=True) * W
    level = jnp.dot(window, power, precision=HIGH, preferred_element_type=jnp.float32) / totals
    gain = lax.rsqrt(level + 1e-06)
    here = slice(m * BLOCK, (m + 1) * BLOCK)
    ahead = jnp.full((BAND_MAX, BLOCK), small[small.shape[0] - 1, 0, 0], jnp.int32) == 0
    for p in range(2):
        for w in range(W):
            at = slice((p * W + w) * BAND_MAX, (p * W + w + 1) * BAND_MAX)
            low = spec[w, p, :BAND_MAX, here].astype(jnp.float32) * gain[:BAND_MAX]
            high = spec[w, p, F - BAND_MAX :, here].astype(jnp.float32) * gain[F - BAND_MAX :]
            cols[m * 2, at] = jnp.where(ahead, low, high).astype(jnp.bfloat16)
            cols[m * 2 + 1, at] = jnp.where(ahead, high, low).astype(jnp.bfloat16)


class Gather:
    def __init__(self, axis, high, low, own, buf, send, recv):
        self.axis, self.high, self.low = axis, high, low
        self.own, self.buf, self.send, self.recv = own, buf, send, recv
        self.me = lax.axis_index(axis)
        self.p, self.l = lax.div(self.me, low), lax.rem(self.me, low)
        p, l = self.p, self.l
        self.dirs = [
            (p + 1 < high, self.me + low),
            (p > 0, self.me - low),
            (l + 1 < low, self.me + 1),
            (l > 0, self.me - 1),
        ]
        if high == 1:
            self.dirs[0] = self.dirs[1] = None
        if low == 1:
            self.dirs[2] = self.dirs[3] = None
        self.closing = False

    def greet(self, barrier):
        for entry in self.dirs:
            if entry is not None:

                @pl.when(entry[0])
                def _():
                    pl.semaphore_signal(
                        barrier, inc=1, device_id={self.axis: entry[1]}, device_id_type=MESH
                    )

    def peers(self):
        return sum(jnp.where(entry[0], 1, 0) for entry in self.dirs if entry is not None)

    def copy(self, way, src, q, own):
        return pltpu.make_async_remote_copy(
            src_ref=self.own.at[q] if own else self.buf.at[src, q],
            dst_ref=self.buf.at[src, q],
            send_sem=self.send.at[way, src, q],
            recv_sem=self.recv.at[src, q],
            device_id={self.axis: self.dirs[way][1]},
            device_id_type=MESH,
        )

    def pass_on(self, ways, src, q, own=False):
        for way in ways:
            if self.dirs[way] is not None:

                @pl.when(self.dirs[way][0])
                def _():
                    piece = self.copy(way, src, q, own)
                    if self.closing:
                        piece.wait_send()
                    else:
                        piece.start()

    def arrive(self, there, src, q, ways, use):
        @pl.when(there)
        def _():
            if not self.closing:
                pltpu.make_async_copy(
                    self.buf.at[src, q], self.buf.at[src, q], self.recv.at[src, q]
                ).wait()
            self.pass_on(ways, src, q)
            if use is not None and not self.closing:
                use(src, q)

    def start(self, q):
        self.pass_on((0, 1, 2, 3), self.me, q, own=True)

    def step(self, st, q, use, low_first=False):
        p, l, low = self.p, self.l, self.low
        turn = () if low_first else (2, 3)
        if 0 < st < self.high:
            self.arrive(p - st >= 0, (p - st) * low + l, q, (0,) + turn, use)
            self.arrive(p + st < self.high, (p + st) * low + l, q, (1,) + turn, use)
        d = st - 1
        if not 0 <= d < self.high:
            return
        for far, way in [(p, None)] if d == 0 else [(p - d, 0), (p + d, 1)]:
            inside = (far >= 0) & (far < self.high)
            for e in range(1, low):
                for there, other, on in ((l - e >= 0, l - e, 2), (l + e < low, l + e, 3)):
                    if not low_first:
                        ways = (on,)
                    elif d == 0:
                        ways = (0, 1, on)
                    else:
                        ways = (way,)
                    self.arrive(inside & there, far * low + other, q, ways, use)


def part_rows(part):
    return pl.ds(part * (DEPTH // PARTS), DEPTH // PARTS)


class Line:
    def __init__(self, low, own, bufs, send, recv):
        self.low, self.own, self.bufs, self.send, self.recv = low, own, bufs, send, recv
        self.me = lax.axis_index("seg")
        self.z = lax.div(self.me, low)
        self.late = lax.rem(lax.axis_index("grp"), CORES) == CORES - 1
        self.turns = low == 2 and CORES == 2
        self.closing = False

    def slot(self, d, way):
        return d if d > 1 else 1 - way

    def buf(self, d, way):
        return self.bufs[self.slot(d, way)]

    def move(self, way, d, q, part):
        at = self.slot(d + 1, way)
        rows = part_rows(part)
        piece = pltpu.make_async_remote_copy(
            src_ref=(self.buf(d, way) if d else self.own).at[q, rows],
            dst_ref=self.bufs[at].at[q, rows],
            send_sem=self.send.at[way, d, q, part],
            recv_sem=self.recv.at[at, q, part],
            device_id={"seg": self.me + (self.low if way else -self.low)},
            device_id_type=MESH,
        )
        if self.closing:
            piece.wait_send()
        else:
            piece.start()

    def start(self, q):
        z = self.z

        @pl.when((z + 1 < LEVELS) & (z != LEVELS - 2))
        def _():
            for part in range(PARTS):
                self.move(1, 0, q, part)

        @pl.when((z > 0) & (z != 1))
        def _():
            for part in range(PARTS):
                self.move(0, 0, q, part)

    def there(self, d):
        z = self.z
        left, right = z - d >= 0, z + d < LEVELS
        on_right, on_left = z + 1 < LEVELS, z > 0
        if d == 1:
            left, right = left & (z != LEVELS - 1), right & (z != 0)
        if self.turns and d == 1:
            first = jnp.logical_not(self.late) & (not self.closing)
            on_right, on_left = on_right & (first | (z != 1)), on_left & (first | (z != LEVELS - 2))
        elif self.turns and d == 2:
            on_right, on_left = on_right & self.late, on_left & self.late
        elif self.turns:
            left, right = left & self.late, right & self.late
        return ((left, z - d, on_right, 1), (right, z + d, on_left, 0))

    def cross(self, q):
        for at, way in ((1, 1), (LEVELS - 2, 0)):

            @pl.when(self.z == at)
            def _():
                for part in range(PARTS):
                    self.move(way, 1, q, part)

    def arrive(self, d, q, then=None):
        for part in range(PARTS):
            for here, _, on, way in self.there(d):

                @pl.when(here)
                def _():
                    if not self.closing:
                        at = self.slot(d, way)
                        piece = self.bufs[at].at[q, part_rows(part)]
                        pltpu.make_async_copy(piece, piece, self.recv.at[at, q, part]).wait()

                    if d + 1 < LEVELS:

                        @pl.when(on)
                        def _():
                            self.move(way, d, q, part)

                    if then is not None:
                        then(q, part)


def kernel(
    nseg, ngrp, small, spec, near, far, cols, left, right, two, three, side, grp_buf, ops, stage, end_stage,
    line_send, line_recv, side_send, side_recv, grp_send, grp_recv,
    far_send, end_send, far_recv, pass_send, pass_recv,
    turn_stage, turn_send, rows_send, rows_recv, go, move,
):
    low = nseg // LEVELS
    slots = far.shape[1]
    line = Line(low, cols, (left, right, two, three), line_send, line_recv)
    grp = Gather("grp", ngrp // CORES, CORES, cols, grp_buf, grp_send, grp_recv)
    me, z = line.me, line.z
    y = lax.rem(me, low)
    mates = [lax.rem(y + e, low) for e in range(1, low)]
    before = lax.rem(y + low - 1, low)
    is_end = (z == 0) | (z == LEVELS - 1)
    inner = (z == 1) | (z == LEVELS - 2)
    end = jnp.where(z == 1, 0, LEVELS - 1)
    beside = jnp.where(z == 0, 1, LEVELS - 2)

    barrier = pltpu.get_barrier_semaphore()

    def greet(seg):
        pl.semaphore_signal(barrier, inc=1, device_id={"seg": seg}, device_id_type=MESH)

    for on, seg in ((z + 1 < LEVELS, me + low), (z > 0, me - low)):

        @pl.when(on)
        def _():
            greet(seg)

    for mate in mates:
        greet(z * low + mate)
        if line.turns:

            @pl.when(is_end)
            def _():
                greet(beside * low + mate)

    late = line.late
    early = jnp.logical_not(late)
    grp.greet(barrier)

    def side_copy(e, q):
        return pltpu.make_async_remote_copy(
            src_ref=cols.at[q],
            dst_ref=side.at[y, q],
            send_sem=side_send.at[e, q],
            recv_sem=side_recv.at[y, q],
            device_id={"seg": z * low + mates[e]},
            device_id_type=MESH,
        )

    def begin(q):
        line.start(q)
        for e in range(low - 1):
            if line.closing:
                side_copy(e, q).wait_send()
            else:
                side_copy(e, q).start()
        grp.start(q)

    def loop(fn, count=PIECES):
        def step(q, carry):
            fn(q)
            return carry

        lax.fori_loop(0, count, step, 0)

    for m in range(BLK_DEV):
        whiten(m, small, spec, cols)
        if m == 0:
            inner_peers = jnp.where(z + 1 < LEVELS, 1, 0) + jnp.where(z > 0, 1, 0)
            if line.turns:
                inner_peers += jnp.where(inner, low - 1, 0)
            pl.semaphore_wait(barrier, inner_peers + (low - 1) + grp.peers())
        begin(2 * m)
        begin(2 * m + 1)

    own = pltpu.make_async_copy(cols, side.at[y], move)
    own.start()

    half = DEPTH // 2

    def operands(slot, q, piece):
        band = lax.rem(q, 2)
        bin_of = lax.rem(lax.broadcasted_iota(jnp.int32, (1, DEPTH), 1), BAND_MAX)
        live = jnp.where(bin_of < small[small.shape[0] - 1, band, 1], 1.0, 0.0).astype(jnp.float32)
        rows = jnp.transpose(piece.astype(jnp.float32)) * live
        ops[slot, q, :BLOCK] = rows.astype(jnp.bfloat16)
        ops[slot, q, BLOCK:, :half] = rows[:, half:].astype(jnp.bfloat16)
        ops[slot, q, BLOCK:, half:] = (-rows[:, :half]).astype(jnp.bfloat16)

    loop(lambda q: operands(y, q, cols[q]))

    def scale(band):
        return lax.rsqrt(jnp.full((1, BLOCK), W * small[small.shape[0] - 1, band, 1], jnp.int32).astype(jnp.float32))

    def near_from(piece, src, q):
        m, band = lax.div(q, 2), lax.rem(q, 2)
        at = pl.ds(pl.multiple_of(src * (BLK_DEV * BLOCK) + m * BLOCK, BLOCK), BLOCK)
        for i in range(BLK_DEV):
            prod = jnp.dot(ops[y, i * 2 + band], piece, preferred_element_type=jnp.float32)
            prod = (prod * scale(band)).astype(jnp.bfloat16)
            near[band, 0, i * BLOCK : (i + 1) * BLOCK, at] = prod[:BLOCK]
            near[band, 1, i * BLOCK : (i + 1) * BLOCK, at] = prod[BLOCK:]

    def use_near(src, q):
        near_from(grp_buf[src, q], src, q)

    loop(lambda q: near_from(cols[q], grp.me, q))

    def pair(owner, slot, src, t, dst, c):
        i, m, band = (small[owner * 3 + k, c, t] for k in range(3))
        factor = jnp.where(c < small[nseg * 3 + lax.div(owner, slots), lax.rem(owner, slots), t], scale(band), 0.0)
        prod = jnp.dot(
            ops[slot, i * 2 + band], src[m * 2 + band], preferred_element_type=jnp.float32
        )
        prod = (prod * factor).astype(jnp.bfloat16)
        dst[c, 0] = prod[:BLOCK]
        dst[c, 1] = prod[BLOCK:]

    def pass_on(q, part):
        rows = part_rows(part)
        piece = pltpu.make_async_remote_copy(
            src_ref=three.at[q, rows],
            dst_ref=left.at[q, rows],
            send_sem=pass_send.at[q, part],
            recv_sem=pass_recv.at[q, part],
            device_id={"seg": z * low + mates[0]},
            device_id_type=MESH,
        )
        if line.closing:
            piece.wait_send()
        else:
            piece.start()

    def passed(q):
        for part in range(PARTS):
            piece = left.at[q, part_rows(part)]
            pltpu.make_async_copy(piece, piece, pass_recv.at[q, part]).wait()

    def level_pairs(buf, src, c, others):
        t = src * low + y
        pair(me, y, buf, t, far.at[t], c)
        for mate in others:
            pair(z * low + mate, mate, buf, t, stage.at[mate, src], c)

    def hand_over(src, others):
        for mate in others:
            piece = pltpu.make_async_remote_copy(
                src_ref=stage.at[mate, src],
                dst_ref=far.at[src * low + y],
                send_sem=far_send.at[mate, src],
                recv_sem=far_recv.at[src * low + y],
                device_id={"seg": z * low + mate},
                device_id_type=MESH,
            )
            if line.closing:
                piece.wait_send()
            else:
                piece.start()

    def end_copy(other):
        return pltpu.make_async_remote_copy(
            src_ref=end_stage.at[other],
            dst_ref=far.at[z * low + other],
            send_sem=end_send.at[other],
            recv_sem=far_recv.at[z * low + other],
            device_id={"seg": end * low + y},
            device_id_type=MESH,
        )

    def for_end():
        for at, buf in ((1, left), (LEVELS - 2, right)):

            @pl.when(z == at)
            def _():
                loop(lambda q: operands(low, q, buf[q]))

        @pl.when(inner)
        def _():
            for other in [y] + mates:
                t = z * low + other
                loop(
                    lambda c: pair(end * low + y, low, side.at[other], t, end_stage.at[other], c),
                    slots,
                )
                end_copy(other).start()

    def rows_copy(q):
        return pltpu.make_async_remote_copy(
            src_ref=side.at[mates[0], q],
            dst_ref=three.at[q],
            send_sem=rows_send.at[q],
            recv_sem=rows_recv.at[q],
            device_id={"seg": beside * low + y},
            device_id_type=MESH,
        )

    def turn_copy(k):
        t = (LEVELS - 1 - end) * low + y
        return pltpu.make_async_remote_copy(
            src_ref=turn_stage.at[k],
            dst_ref=far.at[t],
            send_sem=turn_send.at[k],
            recv_sem=far_recv.at[t],
            device_id={"seg": end * low + (mates[0] if k else y)},
            device_id_type=MESH,
        )

    def turn_pairs():
        t = (LEVELS - 1 - end) * low + y
        for k, owner in enumerate((y, mates[0])):
            loop(
                lambda c: pair(end * low + owner, low + k, two, t, turn_stage.at[k], c), slots
            )

    def take_turn(step):
        pl.semaphore_signal(
            go, inc=1, device_id={"grp": grp.me + step}, device_id_type=MESH
        )

    def first(q):
        line.arrive(1, q)
        grp.step(1, q, None if grp.closing else use_near)
        if not line.closing:
            for mate in mates:
                pltpu.make_async_copy(
                    side.at[mate, q], side.at[mate, q], side_recv.at[mate, q]
                ).wait()
                operands(mate, q, side[mate, q])
        if line.turns:

            @pl.when(is_end & early)
            def _():
                if line.closing:
                    rows_copy(q).wait_send()
                else:
                    rows_copy(q).start()

    def second(q):
        if line.turns and not line.closing:

            @pl.when(inner & early & (q == PIECES - 1))
            def _():
                line.closing = True
                loop(line.cross, PIECES - 1)
                line.closing = False
                take_turn(1)

        line.arrive(2, q)
        grp.step(2, q, None if grp.closing else use_near)
        if line.turns and not line.closing:

            @pl.when(inner & early)
            def _():
                pltpu.make_async_copy(three.at[q], three.at[q], rows_recv.at[q]).wait()
                operands(low + 1, q, three[q])

        if not line.closing:

            @pl.when(q < slots)
            def _():
                for mate in mates:
                    t = z * low + mate
                    pair(me, y, side.at[mate], t, far.at[t], q)
                for here, src, _, way in line.there(1):

                    @pl.when(here)
                    def _():
                        level_pairs(line.buf(1, way), src, q, mates)

                        @pl.when(q == slots - 1)
                        def _():
                            hand_over(src, mates)

    def later(d):
        def step(q):
            if d < LEVELS:
                line.arrive(d, q, pass_on if d == LEVELS - 1 else None)
            grp.step(d, q, None if grp.closing else use_near)

        loop(step)

    def after(d):
        last = d == LEVELS - 1
        others = mates[1:] if last else mates
        for here, src, _, way in line.there(d):

            @pl.when(here)
            def _():
                if not line.closing:
                    loop(lambda c: level_pairs(line.buf(d, way), src, c, others), slots)
                hand_over(src, others)
                if last and not line.closing:
                    loop(passed)
                    t = src * low + before
                    loop(lambda c: pair(me, y, left, t, far.at[t], c), slots)

    loop(first)
    own.wait()
    far[me] = jnp.zeros(far.shape[1:], far.dtype)
    for_end()
    if line.turns:

        @pl.when(inner & late)
        def _():
            pl.semaphore_wait(go, 1)
            loop(line.cross)

    loop(second)
    if line.turns:

        @pl.when(inner & early)
        def _():
            line.closing = True
            line.cross(PIECES - 1)
            line.closing = False
            turn_pairs()
            turn_copy(1).start()

        @pl.when(inner & late)
        def _():
            take_turn(-1)

    after(2)
    if line.turns:

        @pl.when(inner & early)
        def _():
            pl.semaphore_wait(go, 1)
            turn_copy(0).start()

    for d in range(3, max(LEVELS, grp.high + 1)):
        later(d)
        if d < LEVELS:
            after(d)

    line.closing = grp.closing = True
    loop(begin)
    loop(first)
    after(1)
    loop(second)
    after(2)
    for d in range(3, max(LEVELS, grp.high + 1)):
        later(d)
        if d < LEVELS:
            after(d)

    @pl.when(inner)
    def _():
        for other in [y] + mates:
            end_copy(other).wait_send()

    if line.turns:

        @pl.when(inner & late)
        def _():
            loop(line.cross)

        @pl.when(inner & early)
        def _():
            for k in range(2):
                turn_copy(k).wait_send()

    def landed(t):
        tz, ty = lax.div(t, low), lax.rem(t, low)

        across = is_end & (tz == LEVELS - 1 - z)
        passed_on = across & (ty == before)
        handed = is_end & (tz == beside) & (ty == y)
        if line.turns:
            passed_on, handed = passed_on & late, handed | (across & (ty == y) & early)

        @pl.when(handed | ((ty != y) & (tz != z) & jnp.logical_not(passed_on)))
        def _():
            pltpu.make_async_copy(far.at[t], far.at[t], far_recv.at[t]).wait()

    loop(landed, nseg)


def write_kernel(near, far, near_out, far_out, near_sem, far_sem):
    copies = []
    half = far.shape[0] // 2
    for a in range(2):
        for b in range(2):
            copies.append((near.at[a, b], near_out.at[a, b], near_sem.at[a, b]))
        at = pl.ds(a * half, half)
        copies.append((far.at[at], far_out.at[at], far_sem.at[a]))
    copies = [pltpu.make_async_copy(*copy) for copy in copies]
    for copy in copies:
        copy.start()
    for copy in copies:
        copy.wait()


def body(nseg, ngrp, spectra, band_bins, far_list, far_count):
    slots = far_list.shape[3]
    low = nseg // LEVELS
    smem = pl.BlockSpec(memory_space=pltpu.SMEM)
    whole = pl.BlockSpec(memory_space=pltpu.VMEM)
    sems = pltpu.SemaphoreType.DMA
    half = jnp.bfloat16
    lists = jnp.transpose(far_list[0], (0, 3, 2, 1)).reshape(-1, slots, nseg)
    counts = far_count.reshape(-1, slots, nseg)
    bins = jnp.pad(band_bins[None], [(0, 0), (0, slots - 2), (0, nseg - 2)])
    small = jnp.concatenate([lists, counts, bins])
    near = jax.ShapeDtypeStruct((2, 2, BLK_DEV * BLOCK, ngrp * BLK_DEV * BLOCK), half)
    far = jax.ShapeDtypeStruct((nseg, slots, 2, BLOCK, BLOCK), half)
    buffers = [
        pltpu.VMEM((PIECES, DEPTH, BLOCK), half),
        pltpu.VMEM((PIECES, DEPTH, BLOCK), half),
        pltpu.VMEM((PIECES, DEPTH, BLOCK), half),
        pltpu.VMEM((PIECES, DEPTH, BLOCK), half),
        pltpu.VMEM((PIECES, DEPTH, BLOCK), half),
        pltpu.VMEM((low, PIECES, DEPTH, BLOCK), half),
        pltpu.VMEM((ngrp, PIECES, DEPTH, BLOCK), half),
        pltpu.VMEM((low + (2 if low == 2 else 1), PIECES, 2 * BLOCK, DEPTH), half),
        pltpu.VMEM((low, LEVELS, slots, 2, BLOCK, BLOCK), half),
        pltpu.VMEM((low, slots, 2, BLOCK, BLOCK), half),
    ]
    kept = sum(math.prod(a.shape) * 2 for a in buffers + [near, far, spectra])
    vmem = min(kept + 2 * 1024**2, LIMIT)
    near_shape, far_shape = near, far
    near, far = pl.pallas_call(
        functools.partial(kernel, nseg, ngrp),
        out_shape=(near, far),
        in_specs=[smem, whole],
        out_specs=(whole, whole),
        scratch_shapes=buffers
        + [

            sems((2, LEVELS, PIECES, PARTS)),
            sems((LEVELS, PIECES, PARTS)),
            sems((low, PIECES)),
            sems((low, PIECES)),
            sems((4, ngrp, PIECES)),
            sems((ngrp, PIECES)),
            sems((low, LEVELS)),
            sems((low,)),
            sems((nseg,)),
            sems((PIECES, PARTS)),
            sems((PIECES, PARTS)),
            pltpu.VMEM((2, slots, 2, BLOCK, BLOCK), half),
            sems((2,)),
            sems((PIECES,)),
            sems((PIECES,)),
            pltpu.SemaphoreType.REGULAR,
            sems,
        ],
        compiler_params=pltpu.CompilerParams(
            collective_id=0, has_side_effects=True, vmem_limit_bytes=vmem
        ),
    )(small, spectra)
    near, far = pl.pallas_call(
        write_kernel,
        out_shape=(near_shape, far_shape),
        in_specs=[pl.BlockSpec(memory_space=pl.ANY)] * 2,
        out_specs=[pl.BlockSpec(memory_space=pl.ANY)] * 2,
        scratch_shapes=[sems((2, 2)), sems((2,))],
        compiler_params=pltpu.CompilerParams(vmem_limit_bytes=1024**2),
    )(near, far)
    return (near, far[None, None])


def solution(mesh):
    placed = (
        P(None, None, None, ("seg", "grp")),
        P(),
        P("grp", None, None, None, None),
        P("grp", None, None),
    )
    return jax.shard_map(
        functools.partial(body, mesh.shape["seg"], mesh.shape["grp"]),
        mesh=mesh,
        in_specs=placed,
        out_specs=(
            P(None, None, ("seg", "grp"), None),
            P("seg", "grp", None, None, None, None, None),
        ),
        check_vma=False,
    )
```

```python
import functools
import math

import jax
import jax.numpy as jnp
from jax import lax
from jax.experimental import pallas as pl
from jax.experimental.pallas import tpu as pltpu
from jax.sharding import PartitionSpec as P

W = 8
F = 128
BAND_MAX = 48
SMOOTH = 4
BLOCK = 128
BLK_DEV = 3
DEPTH = W * 2 * BAND_MAX
PIECES = 2 * BLK_DEV
LEVELS = 4
PARTS = 2
LIMIT = 62 * 1024**2
CORES = 2


HIGH = lax.Precision.HIGHEST
MESH = pl.DeviceIdType.MESH


def whiten(m, small, spec, cols):
    power = jnp.zeros((F, BLOCK), jnp.float32)
    for w in range(W):
        for p in range(2):
            values = spec[w, p, :, m * BLOCK : (m + 1) * BLOCK].astype(jnp.float32)
            power = power + values * values
    f = lax.broadcasted_iota(jnp.int32, (F, F), 0)
    g = lax.broadcasted_iota(jnp.int32, (F, F), 1)
    window = jnp.where(jnp.abs(f - g) <= SMOOTH, 1.0, 0.0).astype(jnp.float32)
    totals = jnp.sum(window, axis=1, keepdims=True) * W
    level = jnp.dot(window, power, precision=HIGH, preferred_element_type=jnp.float32) / totals
    gain = lax.rsqrt(level + 1e-06)
    here = slice(m * BLOCK, (m + 1) * BLOCK)
    ahead = jnp.full((BAND_MAX, BLOCK), small[small.shape[0] - 1, 0, 0], jnp.int32) == 0
    for p in range(2):
        for w in range(W):
            at = slice((p * W + w) * BAND_MAX, (p * W + w + 1) * BAND_MAX)
            low = spec[w, p, :BAND_MAX, here].astype(jnp.float32) * gain[:BAND_MAX]
            high = spec[w, p, F - BAND_MAX :, here].astype(jnp.float32) * gain[F - BAND_MAX :]
            cols[m * 2, at] = jnp.where(ahead, low, high).astype(jnp.bfloat16)
            cols[m * 2 + 1, at] = jnp.where(ahead, high, low).astype(jnp.bfloat16)


class Gather:
    def __init__(self, axis, high, low, own, buf, send, recv):
        self.axis, self.high, self.low = axis, high, low
        self.own, self.buf, self.send, self.recv = own, buf, send, recv
        self.me = lax.axis_index(axis)
        self.p, self.l = lax.div(self.me, low), lax.rem(self.me, low)
        p, l = self.p, self.l
        self.dirs = [
            (p + 1 < high, self.me + low),
            (p > 0, self.me - low),
            (l + 1 < low, self.me + 1),
            (l > 0, self.me - 1),
        ]
        if high == 1:
            self.dirs[0] = self.dirs[1] = None
        if low == 1:
            self.dirs[2] = self.dirs[3] = None
        self.closing = False

    def greet(self, barrier):
        for entry in self.dirs:
            if entry is not None:

                @pl.when(entry[0])
                def _():
                    pl.semaphore_signal(
                        barrier, inc=1, device_id={self.axis: entry[1]}, device_id_type=MESH
                    )

    def peers(self):
        return sum(jnp.where(entry[0], 1, 0) for entry in self.dirs if entry is not None)

    def copy(self, way, src, q, own):
        return pltpu.make_async_remote_copy(
            src_ref=self.own.at[q] if own else self.buf.at[src, q],
            dst_ref=self.buf.at[src, q],
            send_sem=self.send.at[way, src, q],
            recv_sem=self.recv.at[src, q],
            device_id={self.axis: self.dirs[way][1]},
            device_id_type=MESH,
        )

    def pass_on(self, ways, src, q, own=False):
        for way in ways:
            if self.dirs[way] is not None:

                @pl.when(self.dirs[way][0])
                def _():
                    piece = self.copy(way, src, q, own)
                    if self.closing:
                        piece.wait_send()
                    else:
                        piece.start()

    def arrive(self, there, src, q, ways, use):
        @pl.when(there)
        def _():
            if not self.closing:
                pltpu.make_async_copy(
                    self.buf.at[src, q], self.buf.at[src, q], self.recv.at[src, q]
                ).wait()
            self.pass_on(ways, src, q)
            if use is not None and not self.closing:
                use(src, q)

    def start(self, q):
        self.pass_on((0, 1, 2, 3), self.me, q, own=True)

    def step(self, st, q, use, low_first=False):
        p, l, low = self.p, self.l, self.low
        turn = () if low_first else (2, 3)
        if 0 < st < self.high:
            self.arrive(p - st >= 0, (p - st) * low + l, q, (0,) + turn, use)
            self.arrive(p + st < self.high, (p + st) * low + l, q, (1,) + turn, use)
        d = st - 1
        if not 0 <= d < self.high:
            return
        for far, way in [(p, None)] if d == 0 else [(p - d, 0), (p + d, 1)]:
            inside = (far >= 0) & (far < self.high)
            for e in range(1, low):
                for there, other, on in ((l - e >= 0, l - e, 2), (l + e < low, l + e, 3)):
                    if not low_first:
                        ways = (on,)
                    elif d == 0:
                        ways = (0, 1, on)
                    else:
                        ways = (way,)
                    self.arrive(inside & there, far * low + other, q, ways, use)


def part_rows(part):
    return pl.ds(part * (DEPTH // PARTS), DEPTH // PARTS)


class Line:
    def __init__(self, low, own, bufs, send, recv):
        self.low, self.own, self.bufs, self.send, self.recv = low, own, bufs, send, recv
        self.me = lax.axis_index("seg")
        self.z = lax.div(self.me, low)
        self.late = lax.rem(lax.axis_index("grp"), CORES) == CORES - 1
        self.turns = low == 2 and CORES == 2
        self.closing = False

    def slot(self, d, way):
        return d if d > 1 else 1 - way

    def buf(self, d, way):
        return self.bufs[self.slot(d, way)]

    def move(self, way, d, q, part):
        at = self.slot(d + 1, way)
        rows = part_rows(part)
        piece = pltpu.make_async_remote_copy(
            src_ref=(self.buf(d, way) if d else self.own).at[q, rows],
            dst_ref=self.bufs[at].at[q, rows],
            send_sem=self.send.at[way, d, q, part],
            recv_sem=self.recv.at[at, q, part],
            device_id={"seg": self.me + (self.low if way else -self.low)},
            device_id_type=MESH,
        )
        if self.closing:
            piece.wait_send()
        else:
            piece.start()

    def start(self, q):
        z = self.z

        @pl.when((z + 1 < LEVELS) & (z != LEVELS - 2))
        def _():
            for part in range(PARTS):
                self.move(1, 0, q, part)

        @pl.when((z > 0) & (z != 1))
        def _():
            for part in range(PARTS):
                self.move(0, 0, q, part)

    def there(self, d):
        z = self.z
        left, right = z - d >= 0, z + d < LEVELS
        on_right, on_left = z + 1 < LEVELS, z > 0
        if d == 1:
            left, right = left & (z != LEVELS - 1), right & (z != 0)
        if self.turns and d == 1:
            first = jnp.logical_not(self.late) & (not self.closing)
            on_right, on_left = on_right & (first | (z != 1)), on_left & (first | (z != LEVELS - 2))
        elif self.turns and d == 2:
            on_right, on_left = on_right & self.late, on_left & self.late
        elif self.turns:
            left, right = left & self.late, right & self.late
        return ((left, z - d, on_right, 1), (right, z + d, on_left, 0))

    def cross(self, q):
        for at, way in ((1, 1), (LEVELS - 2, 0)):

            @pl.when(self.z == at)
            def _():
                for part in range(PARTS):
                    self.move(way, 1, q, part)

    def arrive(self, d, q, then=None):
        for part in range(PARTS):
            for here, _, on, way in self.there(d):

                @pl.when(here)
                def _():
                    if not self.closing:
                        at = self.slot(d, way)
                        piece = self.bufs[at].at[q, part_rows(part)]
                        pltpu.make_async_copy(piece, piece, self.recv.at[at, q, part]).wait()

                    if d + 1 < LEVELS:

                        @pl.when(on)
                        def _():
                            self.move(way, d, q, part)

                    if then is not None:
                        then(q, part)


def kernel(
    nseg, ngrp, small, spec, near, far, cols, left, right, two, three, side, grp_buf, ops, stage, end_stage,
    line_send, line_recv, side_send, side_recv, grp_send, grp_recv,
    far_send, end_send, far_recv, pass_send, pass_recv,
    turn_stage, turn_send, rows_send, rows_recv, go, move,
):
    low = nseg // LEVELS
    slots = far.shape[1]
    line = Line(low, cols, (left, right, two, three), line_send, line_recv)
    grp = Gather("grp", ngrp // CORES, CORES, cols, grp_buf, grp_send, grp_recv)
    me, z = line.me, line.z
    y = lax.rem(me, low)
    mates = [lax.rem(y + e, low) for e in range(1, low)]
    before = lax.rem(y + low - 1, low)
    is_end = (z == 0) | (z == LEVELS - 1)
    inner = (z == 1) | (z == LEVELS - 2)
    end = jnp.where(z == 1, 0, LEVELS - 1)
    beside = jnp.where(z == 0, 1, LEVELS - 2)

    barrier = pltpu.get_barrier_semaphore()

    def greet(seg):
        pl.semaphore_signal(barrier, inc=1, device_id={"seg": seg}, device_id_type=MESH)

    for on, seg in ((z + 1 < LEVELS, me + low), (z > 0, me - low)):

        @pl.when(on)
        def _():
            greet(seg)

    for mate in mates:
        greet(z * low + mate)
        if line.turns:

            @pl.when(is_end)
            def _():
                greet(beside * low + mate)

    late = line.late
    early = jnp.logical_not(late)
    grp.greet(barrier)

    def side_copy(e, q):
        return pltpu.make_async_remote_copy(
            src_ref=cols.at[q],
            dst_ref=side.at[y, q],
            send_sem=side_send.at[e, q],
            recv_sem=side_recv.at[y, q],
            device_id={"seg": z * low + mates[e]},
            device_id_type=MESH,
        )

    def begin(q):
        line.start(q)
        for e in range(low - 1):
            if line.closing:
                side_copy(e, q).wait_send()
            else:
                side_copy(e, q).start()
        grp.start(q)

    def loop(fn, count=PIECES):
        def step(q, carry):
            fn(q)
            return carry

        lax.fori_loop(0, count, step, 0)

    for m in range(BLK_DEV):
        whiten(m, small, spec, cols)
        if m == 0:
            inner_peers = jnp.where(z + 1 < LEVELS, 1, 0) + jnp.where(z > 0, 1, 0)
            if line.turns:
                inner_peers += jnp.where(inner, low - 1, 0)
            pl.semaphore_wait(barrier, inner_peers + (low - 1) + grp.peers())
        begin(2 * m)
        begin(2 * m + 1)

    own = pltpu.make_async_copy(cols, side.at[y], move)
    own.start()

    half = DEPTH // 2

    def operands(slot, q, piece):
        band = lax.rem(q, 2)
        bin_of = lax.rem(lax.broadcasted_iota(jnp.int32, (1, DEPTH), 1), BAND_MAX)
        live = jnp.where(bin_of < small[small.shape[0] - 1, band, 1], 1.0, 0.0).astype(jnp.float32)
        rows = jnp.transpose(piece.astype(jnp.float32)) * live
        ops[slot, q, :BLOCK] = rows.astype(jnp.bfloat16)
        ops[slot, q, BLOCK:, :half] = rows[:, half:].astype(jnp.bfloat16)
        ops[slot, q, BLOCK:, half:] = (-rows[:, :half]).astype(jnp.bfloat16)

    loop(lambda q: operands(y, q, cols[q]))

    def scale(band):
        return lax.rsqrt(jnp.full((1, BLOCK), W * small[small.shape[0] - 1, band, 1], jnp.int32).astype(jnp.float32))

    def near_from(piece, src, q):
        m, band = lax.div(q, 2), lax.rem(q, 2)
        at = pl.ds(pl.multiple_of(src * (BLK_DEV * BLOCK) + m * BLOCK, BLOCK), BLOCK)
        for i in range(BLK_DEV):
            prod = jnp.dot(ops[y, i * 2 + band], piece, preferred_element_type=jnp.float32)
            prod = (prod * scale(band)).astype(jnp.bfloat16)
            near[band, 0, i * BLOCK : (i + 1) * BLOCK, at] = prod[:BLOCK]
            near[band, 1, i * BLOCK : (i + 1) * BLOCK, at] = prod[BLOCK:]

    def use_near(src, q):
        near_from(grp_buf[src, q], src, q)

    loop(lambda q: near_from(cols[q], grp.me, q))

    def pair(owner, slot, src, t, dst, c):
        i, m, band = (small[owner * 3 + k, c, t] for k in range(3))
        factor = jnp.where(c < small[nseg * 3 + lax.div(owner, slots), lax.rem(owner, slots), t], scale(band), 0.0)
        prod = jnp.dot(
            ops[slot, i * 2 + band], src[m * 2 + band], preferred_element_type=jnp.float32
        )
        prod = (prod * factor).astype(jnp.bfloat16)
        dst[c, 0] = prod[:BLOCK]
        dst[c, 1] = prod[BLOCK:]

    def pass_on(q, part):
        rows = part_rows(part)
        piece = pltpu.make_async_remote_copy(
            src_ref=three.at[q, rows],
            dst_ref=left.at[q, rows],
            send_sem=pass_send.at[q, part],
            recv_sem=pass_recv.at[q, part],
            device_id={"seg": z * low + mates[0]},
            device_id_type=MESH,
        )
        if line.closing:
            piece.wait_send()
        else:
            piece.start()

    def passed(q):
        for part in range(PARTS):
            piece = left.at[q, part_rows(part)]
            pltpu.make_async_copy(piece, piece, pass_recv.at[q, part]).wait()

    def level_pairs(buf, src, c, others, own=True):
        t = src * low + y
        for mate in others:
            pair(z * low + mate, mate, buf, t, stage.at[mate, src], c)
        if own:
            pair(me, y, buf, t, far.at[t], c)

    def hand_over(src, others):
        for mate in others:
            piece = pltpu.make_async_remote_copy(
                src_ref=stage.at[mate, src],
                dst_ref=far.at[src * low + y],
                send_sem=far_send.at[mate, src],
                recv_sem=far_recv.at[src * low + y],
                device_id={"seg": z * low + mate},
                device_id_type=MESH,
            )
            if line.closing:
                piece.wait_send()
            else:
                piece.start()

    def end_copy(other):
        return pltpu.make_async_remote_copy(
            src_ref=end_stage.at[other],
            dst_ref=far.at[z * low + other],
            send_sem=end_send.at[other],
            recv_sem=far_recv.at[z * low + other],
            device_id={"seg": end * low + y},
            device_id_type=MESH,
        )

    def for_end():
        for at, buf in ((1, left), (LEVELS - 2, right)):

            @pl.when(z == at)
            def _():
                loop(lambda q: operands(low, q, buf[q]))

        @pl.when(inner)
        def _():
            for other in [y] + mates:
                t = z * low + other
                loop(
                    lambda c: pair(end * low + y, low, side.at[other], t, end_stage.at[other], c),
                    slots,
                )
                end_copy(other).start()

    def rows_copy(q):
        return pltpu.make_async_remote_copy(
            src_ref=side.at[mates[0], q],
            dst_ref=three.at[q],
            send_sem=rows_send.at[q],
            recv_sem=rows_recv.at[q],
            device_id={"seg": beside * low + y},
            device_id_type=MESH,
        )

    def turn_copy(k):
        t = (LEVELS - 1 - end) * low + y
        return pltpu.make_async_remote_copy(
            src_ref=turn_stage.at[k],
            dst_ref=far.at[t],
            send_sem=turn_send.at[k],
            recv_sem=far_recv.at[t],
            device_id={"seg": end * low + (mates[0] if k else y)},
            device_id_type=MESH,
        )

    def turn_pairs():
        t = (LEVELS - 1 - end) * low + y
        for k, owner in enumerate((y, mates[0])):
            loop(
                lambda c: pair(end * low + owner, low + k, two, t, turn_stage.at[k], c), slots
            )

    def take_turn(step):
        pl.semaphore_signal(
            go, inc=1, device_id={"grp": grp.me + step}, device_id_type=MESH
        )

    def first(q):
        line.arrive(1, q)
        grp.step(1, q, None if grp.closing else use_near)
        if not line.closing:
            for mate in mates:
                pltpu.make_async_copy(
                    side.at[mate, q], side.at[mate, q], side_recv.at[mate, q]
                ).wait()
                operands(mate, q, side[mate, q])
        if line.turns:

            @pl.when(is_end & early)
            def _():
                if line.closing:
                    rows_copy(q).wait_send()
                else:
                    rows_copy(q).start()

    def second(q):
        if line.turns and not line.closing:

            @pl.when(inner & early & (q == PIECES - 3))
            def _():
                line.closing = True
                loop(line.cross, PIECES - 3)
                line.closing = False
                take_turn(1)

        line.arrive(2, q)
        grp.step(2, q, None if grp.closing else use_near)
        if line.turns and not line.closing:

            @pl.when(inner & early)
            def _():
                pltpu.make_async_copy(three.at[q], three.at[q], rows_recv.at[q]).wait()
                operands(low + 1, q, three[q])

        if not line.closing:

            @pl.when(q < slots)
            def _():
                for mate in mates:
                    t = z * low + mate
                    pair(me, y, side.at[mate], t, far.at[t], q)
                for here, src, _, way in line.there(1):

                    @pl.when(here)
                    def _():
                        level_pairs(line.buf(1, way), src, q, mates)

                        @pl.when(q == slots - 1)
                        def _():
                            hand_over(src, mates)

    def later(d):
        def step(q):
            if d < LEVELS:
                line.arrive(d, q, pass_on if d == LEVELS - 1 else None)
            grp.step(d, q, None if grp.closing else use_near)

        loop(step)

    def after(d):
        last = d == LEVELS - 1
        others = mates[1:] if last else mates
        for here, src, _, way in line.there(d):

            @pl.when(here)
            def _():
                if not line.closing:
                    if others:
                        loop(lambda c: level_pairs(line.buf(d, way), src, c, others, False), slots)
                hand_over(src, others)
                if not line.closing:
                    loop(lambda c: level_pairs(line.buf(d, way), src, c, ()), slots)
                if last and not line.closing:
                    loop(passed)
                    t = src * low + before
                    loop(lambda c: pair(me, y, left, t, far.at[t], c), slots)

    loop(first)
    own.wait()
    far[me] = jnp.zeros(far.shape[1:], far.dtype)
    for_end()
    if line.turns:

        @pl.when(inner & late)
        def _():
            pl.semaphore_wait(go, 1)
            loop(line.cross)

    loop(second)
    if line.turns:

        @pl.when(inner & early)
        def _():
            line.closing = True
            line.cross(PIECES - 3)
            line.cross(PIECES - 2)
            line.cross(PIECES - 1)
            line.closing = False
            turn_pairs()

        @pl.when(inner & late)
        def _():
            take_turn(-1)

    after(2)
    if line.turns:

        @pl.when(inner & early)
        def _():
            pl.semaphore_wait(go, 1)
            turn_copy(1).start()
            turn_copy(0).start()

    for d in range(3, max(LEVELS, grp.high + 1)):
        later(d)
        if d < LEVELS:
            after(d)

    line.closing = grp.closing = True
    loop(begin)
    loop(first)
    after(1)
    loop(second)
    after(2)
    for d in range(3, max(LEVELS, grp.high + 1)):
        later(d)
        if d < LEVELS:
            after(d)

    @pl.when(inner)
    def _():
        for other in [y] + mates:
            end_copy(other).wait_send()

    if line.turns:

        @pl.when(inner & late)
        def _():
            loop(line.cross)

        @pl.when(inner & early)
        def _():
            for k in range(2):
                turn_copy(k).wait_send()

    def landed(t):
        tz, ty = lax.div(t, low), lax.rem(t, low)

        across = is_end & (tz == LEVELS - 1 - z)
        passed_on = across & (ty == before)
        handed = is_end & (tz == beside) & (ty == y)
        if line.turns:
            passed_on, handed = passed_on & late, handed | (across & (ty == y) & early)

        @pl.when(handed | ((ty != y) & (tz != z) & jnp.logical_not(passed_on)))
        def _():
            pltpu.make_async_copy(far.at[t], far.at[t], far_recv.at[t]).wait()

    loop(landed, nseg)


def write_kernel(near, far, near_out, far_out, near_sem, far_sem):
    copies = []
    half = far.shape[0] // 2
    for a in range(2):
        for b in range(2):
            copies.append((near.at[a, b], near_out.at[a, b], near_sem.at[a, b]))
        at = pl.ds(a * half, half)
        copies.append((far.at[at], far_out.at[at], far_sem.at[a]))
    copies = [pltpu.make_async_copy(*copy) for copy in copies]
    for copy in copies:
        copy.start()
    for copy in copies:
        copy.wait()


def body(nseg, ngrp, spectra, band_bins, far_list, far_count):
    slots = far_list.shape[3]
    low = nseg // LEVELS
    smem = pl.BlockSpec(memory_space=pltpu.SMEM)
    whole = pl.BlockSpec(memory_space=pltpu.VMEM)
    sems = pltpu.SemaphoreType.DMA
    half = jnp.bfloat16
    lists = jnp.transpose(far_list[0], (0, 3, 2, 1)).reshape(-1, slots, nseg)
    counts = far_count.reshape(-1, slots, nseg)
    bins = jnp.pad(band_bins[None], [(0, 0), (0, slots - 2), (0, nseg - 2)])
    small = jnp.concatenate([lists, counts, bins])
    near = jax.ShapeDtypeStruct((2, 2, BLK_DEV * BLOCK, ngrp * BLK_DEV * BLOCK), half)
    far = jax.ShapeDtypeStruct((nseg, slots, 2, BLOCK, BLOCK), half)
    buffers = [
        pltpu.VMEM((PIECES, DEPTH, BLOCK), half),
        pltpu.VMEM((PIECES, DEPTH, BLOCK), half),
        pltpu.VMEM((PIECES, DEPTH, BLOCK), half),
        pltpu.VMEM((PIECES, DEPTH, BLOCK), half),
        pltpu.VMEM((PIECES, DEPTH, BLOCK), half),
        pltpu.VMEM((low, PIECES, DEPTH, BLOCK), half),
        pltpu.VMEM((ngrp, PIECES, DEPTH, BLOCK), half),
        pltpu.VMEM((low + (2 if low == 2 else 1), PIECES, 2 * BLOCK, DEPTH), half),
        pltpu.VMEM((low, LEVELS, slots, 2, BLOCK, BLOCK), half),
        pltpu.VMEM((low, slots, 2, BLOCK, BLOCK), half),
    ]
    kept = sum(math.prod(a.shape) * 2 for a in buffers + [near, far, spectra])
    vmem = min(kept + 2 * 1024**2, LIMIT)
    near_shape, far_shape = near, far
    near, far = pl.pallas_call(
        functools.partial(kernel, nseg, ngrp),
        out_shape=(near, far),
        in_specs=[smem, whole],
        out_specs=(whole, whole),
        scratch_shapes=buffers
        + [

            sems((2, LEVELS, PIECES, PARTS)),
            sems((LEVELS, PIECES, PARTS)),
            sems((low, PIECES)),
            sems((low, PIECES)),
            sems((4, ngrp, PIECES)),
            sems((ngrp, PIECES)),
            sems((low, LEVELS)),
            sems((low,)),
            sems((nseg,)),
            sems((PIECES, PARTS)),
            sems((PIECES, PARTS)),
            pltpu.VMEM((2, slots, 2, BLOCK, BLOCK), half),
            sems((2,)),
            sems((PIECES,)),
            sems((PIECES,)),
            pltpu.SemaphoreType.REGULAR,
            sems,
        ],
        compiler_params=pltpu.CompilerParams(
            collective_id=0, has_side_effects=True, vmem_limit_bytes=vmem
        ),
    )(small, spectra)
    near, far = pl.pallas_call(
        write_kernel,
        out_shape=(near_shape, far_shape),
        in_specs=[pl.BlockSpec(memory_space=pl.ANY)] * 2,
        out_specs=[pl.BlockSpec(memory_space=pl.ANY)] * 2,
        scratch_shapes=[sems((2, 2)), sems((2,))],
        compiler_params=pltpu.CompilerParams(vmem_limit_bytes=1024**2),
    )(near, far)
    return (near, far[None, None])


def solution(mesh):
    placed = (
        P(None, None, None, ("seg", "grp")),
        P(),
        P("grp", None, None, None, None),
        P("grp", None, None),
    )
    return jax.shard_map(
        functools.partial(body, mesh.shape["seg"], mesh.shape["grp"]),
        mesh=mesh,
        in_specs=placed,
        out_specs=(
            P(None, None, ("seg", "grp"), None),
            P("seg", "grp", None, None, None, None, None),
        ),
        check_vma=False,
    )
```

```python
import functools
import math

import jax
import jax.numpy as jnp
from jax import lax
from jax.experimental import pallas as pl
from jax.experimental.pallas import tpu as pltpu
from jax.sharding import PartitionSpec as P

W = 8
F = 128
BAND_MAX = 48
SMOOTH = 4
BLOCK = 128
BLK_DEV = 3
DEPTH = W * 2 * BAND_MAX
PIECES = 2 * BLK_DEV
LEVELS = 4
PARTS = 2
LIMIT = 62 * 1024**2
CORES = 2


HIGH = lax.Precision.HIGHEST
MESH = pl.DeviceIdType.MESH


def whiten(m, small, spec, cols):
    power = jnp.zeros((F, BLOCK), jnp.float32)
    for w in range(W):
        for p in range(2):
            values = spec[w, p, :, m * BLOCK : (m + 1) * BLOCK].astype(jnp.float32)
            power = power + values * values
    f = lax.broadcasted_iota(jnp.int32, (F, F), 0)
    g = lax.broadcasted_iota(jnp.int32, (F, F), 1)
    window = jnp.where(jnp.abs(f - g) <= SMOOTH, 1.0, 0.0).astype(jnp.float32)
    totals = jnp.sum(window, axis=1, keepdims=True) * W
    level = jnp.dot(window, power, precision=HIGH, preferred_element_type=jnp.float32) / totals
    gain = lax.rsqrt(level + 1e-06)
    here = slice(m * BLOCK, (m + 1) * BLOCK)
    ahead = jnp.full((BAND_MAX, BLOCK), small[small.shape[0] - 1, 0, 0], jnp.int32) == 0
    for p in range(2):
        for w in range(W):
            at = slice((p * W + w) * BAND_MAX, (p * W + w + 1) * BAND_MAX)
            low = spec[w, p, :BAND_MAX, here].astype(jnp.float32) * gain[:BAND_MAX]
            high = spec[w, p, F - BAND_MAX :, here].astype(jnp.float32) * gain[F - BAND_MAX :]
            cols[m * 2, at] = jnp.where(ahead, low, high).astype(jnp.bfloat16)
            cols[m * 2 + 1, at] = jnp.where(ahead, high, low).astype(jnp.bfloat16)


class Gather:
    def __init__(self, axis, high, low, own, buf, send, recv):
        self.axis, self.high, self.low = axis, high, low
        self.own, self.buf, self.send, self.recv = own, buf, send, recv
        self.me = lax.axis_index(axis)
        self.p, self.l = lax.div(self.me, low), lax.rem(self.me, low)
        p, l = self.p, self.l
        self.dirs = [
            (p + 1 < high, self.me + low),
            (p > 0, self.me - low),
            (l + 1 < low, self.me + 1),
            (l > 0, self.me - 1),
        ]
        if high == 1:
            self.dirs[0] = self.dirs[1] = None
        if low == 1:
            self.dirs[2] = self.dirs[3] = None
        self.closing = False

    def greet(self, barrier):
        for entry in self.dirs:
            if entry is not None:

                @pl.when(entry[0])
                def _():
                    pl.semaphore_signal(
                        barrier, inc=1, device_id={self.axis: entry[1]}, device_id_type=MESH
                    )

    def peers(self):
        return sum(jnp.where(entry[0], 1, 0) for entry in self.dirs if entry is not None)

    def copy(self, way, src, q, own):
        return pltpu.make_async_remote_copy(
            src_ref=self.own.at[q] if own else self.buf.at[src, q],
            dst_ref=self.buf.at[src, q],
            send_sem=self.send.at[way, src, q],
            recv_sem=self.recv.at[src, q],
            device_id={self.axis: self.dirs[way][1]},
            device_id_type=MESH,
        )

    def pass_on(self, ways, src, q, own=False):
        for way in ways:
            if self.dirs[way] is not None:

                @pl.when(self.dirs[way][0])
                def _():
                    piece = self.copy(way, src, q, own)
                    if self.closing:
                        piece.wait_send()
                    else:
                        piece.start()

    def arrive(self, there, src, q, ways, use):
        @pl.when(there)
        def _():
            if not self.closing:
                pltpu.make_async_copy(
                    self.buf.at[src, q], self.buf.at[src, q], self.recv.at[src, q]
                ).wait()
            self.pass_on(ways, src, q)
            if use is not None and not self.closing:
                use(src, q)

    def start(self, q):
        self.pass_on((0, 1, 2, 3), self.me, q, own=True)

    def step(self, st, q, use, low_first=False):
        p, l, low = self.p, self.l, self.low
        turn = () if low_first else (2, 3)
        if 0 < st < self.high:
            self.arrive(p - st >= 0, (p - st) * low + l, q, (0,) + turn, use)
            self.arrive(p + st < self.high, (p + st) * low + l, q, (1,) + turn, use)
        d = st - 1
        if not 0 <= d < self.high:
            return
        for far, way in [(p, None)] if d == 0 else [(p - d, 0), (p + d, 1)]:
            inside = (far >= 0) & (far < self.high)
            for e in range(1, low):
                for there, other, on in ((l - e >= 0, l - e, 2), (l + e < low, l + e, 3)):
                    if not low_first:
                        ways = (on,)
                    elif d == 0:
                        ways = (0, 1, on)
                    else:
                        ways = (way,)
                    self.arrive(inside & there, far * low + other, q, ways, use)


def part_rows(part):
    return pl.ds(part * (DEPTH // PARTS), DEPTH // PARTS)


class Line:
    def __init__(self, low, own, bufs, send, recv):
        self.low, self.own, self.bufs, self.send, self.recv = low, own, bufs, send, recv
        self.me = lax.axis_index("seg")
        self.z = lax.div(self.me, low)
        self.late = lax.rem(lax.axis_index("grp"), CORES) == CORES - 1
        self.turns = low == 2 and CORES == 2
        self.closing = False

    def slot(self, d, way):
        return d if d > 1 else 1 - way

    def buf(self, d, way):
        return self.bufs[self.slot(d, way)]

    def move(self, way, d, q, part):
        at = self.slot(d + 1, way)
        rows = part_rows(part)
        piece = pltpu.make_async_remote_copy(
            src_ref=(self.buf(d, way) if d else self.own).at[q, rows],
            dst_ref=self.bufs[at].at[q, rows],
            send_sem=self.send.at[way, d, q, part],
            recv_sem=self.recv.at[at, q, part],
            device_id={"seg": self.me + (self.low if way else -self.low)},
            device_id_type=MESH,
        )
        if self.closing:
            piece.wait_send()
        else:
            piece.start()

    def start(self, q):
        z = self.z

        @pl.when((z + 1 < LEVELS) & (z != LEVELS - 2))
        def _():
            for part in range(PARTS):
                self.move(1, 0, q, part)

        @pl.when((z > 0) & (z != 1))
        def _():
            for part in range(PARTS):
                self.move(0, 0, q, part)

    def there(self, d):
        z = self.z
        left, right = z - d >= 0, z + d < LEVELS
        on_right, on_left = z + 1 < LEVELS, z > 0
        if d == 1:
            left, right = left & (z != LEVELS - 1), right & (z != 0)
        if self.turns and d == 1:
            first = jnp.logical_not(self.late) & (not self.closing)
            on_right, on_left = on_right & (first | (z != 1)), on_left & (first | (z != LEVELS - 2))
        elif self.turns and d == 2:
            on_right, on_left = on_right & self.late, on_left & self.late
        elif self.turns:
            left, right = left & self.late, right & self.late
        return ((left, z - d, on_right, 1), (right, z + d, on_left, 0))

    def cross(self, q):
        for at, way in ((1, 1), (LEVELS - 2, 0)):

            @pl.when(self.z == at)
            def _():
                for part in range(PARTS):
                    self.move(way, 1, q, part)

    def arrive(self, d, q, then=None):
        for part in range(PARTS):
            for here, _, on, way in self.there(d):

                @pl.when(here)
                def _():
                    if not self.closing:
                        at = self.slot(d, way)
                        piece = self.bufs[at].at[q, part_rows(part)]
                        pltpu.make_async_copy(piece, piece, self.recv.at[at, q, part]).wait()

                    if d + 1 < LEVELS:

                        @pl.when(on)
                        def _():
                            self.move(way, d, q, part)

                    if then is not None:
                        then(q, part)


def kernel(
    nseg, ngrp, small, spec, near, far, cols, left, right, two, three, side, grp_buf, ops, stage, end_stage,
    line_send, line_recv, side_send, side_recv, grp_send, grp_recv,
    far_send, end_send, far_recv, pass_send, pass_recv,
    turn_stage, turn_send, rows_send, rows_recv, go, move,
):
    low = nseg // LEVELS
    slots = far.shape[1]
    line = Line(low, cols, (left, right, two, three), line_send, line_recv)
    grp = Gather("grp", ngrp // CORES, CORES, cols, grp_buf, grp_send, grp_recv)
    me, z = line.me, line.z
    y = lax.rem(me, low)
    mates = [lax.rem(y + e, low) for e in range(1, low)]
    before = lax.rem(y + low - 1, low)
    is_end = (z == 0) | (z == LEVELS - 1)
    inner = (z == 1) | (z == LEVELS - 2)
    end = jnp.where(z == 1, 0, LEVELS - 1)
    beside = jnp.where(z == 0, 1, LEVELS - 2)

    barrier = pltpu.get_barrier_semaphore()

    def greet(seg):
        pl.semaphore_signal(barrier, inc=1, device_id={"seg": seg}, device_id_type=MESH)

    for on, seg in ((z + 1 < LEVELS, me + low), (z > 0, me - low)):

        @pl.when(on)
        def _():
            greet(seg)

    for mate in mates:
        greet(z * low + mate)
        if line.turns:

            @pl.when(is_end)
            def _():
                greet(beside * low + mate)

    late = line.late
    early = jnp.logical_not(late)
    grp.greet(barrier)

    def side_copy(e, q):
        return pltpu.make_async_remote_copy(
            src_ref=cols.at[q],
            dst_ref=side.at[y, q],
            send_sem=side_send.at[e, q],
            recv_sem=side_recv.at[y, q],
            device_id={"seg": z * low + mates[e]},
            device_id_type=MESH,
        )

    def begin(q):
        line.start(q)
        for e in range(low - 1):
            if line.closing:
                side_copy(e, q).wait_send()
            else:
                side_copy(e, q).start()
        grp.start(q)

    def loop(fn, count=PIECES):
        def step(q, carry):
            fn(q)
            return carry

        lax.fori_loop(0, count, step, 0)

    for m in range(BLK_DEV):
        whiten(m, small, spec, cols)
        if m == 0:
            inner_peers = jnp.where(z + 1 < LEVELS, 1, 0) + jnp.where(z > 0, 1, 0)
            if line.turns:
                inner_peers += jnp.where(inner, low - 1, 0)
            pl.semaphore_wait(barrier, inner_peers + (low - 1) + grp.peers())
        begin(2 * m)
        begin(2 * m + 1)

    own = pltpu.make_async_copy(cols, side.at[y], move)
    own.start()

    half = DEPTH // 2

    def operands(slot, q, piece):
        band = lax.rem(q, 2)
        bin_of = lax.rem(lax.broadcasted_iota(jnp.int32, (1, DEPTH), 1), BAND_MAX)
        live = jnp.where(bin_of < small[small.shape[0] - 1, band, 1], 1.0, 0.0).astype(jnp.float32)
        rows = jnp.transpose(piece.astype(jnp.float32)) * live
        ops[slot, q, :BLOCK] = rows.astype(jnp.bfloat16)
        ops[slot, q, BLOCK:, :half] = rows[:, half:].astype(jnp.bfloat16)
        ops[slot, q, BLOCK:, half:] = (-rows[:, :half]).astype(jnp.bfloat16)

    loop(lambda q: operands(y, q, cols[q]))

    def scale(band):
        return lax.rsqrt(jnp.full((1, BLOCK), W * small[small.shape[0] - 1, band, 1], jnp.int32).astype(jnp.float32))

    def near_from(piece, src, q):
        m, band = lax.div(q, 2), lax.rem(q, 2)
        at = pl.ds(pl.multiple_of(src * (BLK_DEV * BLOCK) + m * BLOCK, BLOCK), BLOCK)
        for i in range(BLK_DEV):
            prod = jnp.dot(ops[y, i * 2 + band], piece, preferred_element_type=jnp.float32)
            prod = (prod * scale(band)).astype(jnp.bfloat16)
            near[band, 0, i * BLOCK : (i + 1) * BLOCK, at] = prod[:BLOCK]
            near[band, 1, i * BLOCK : (i + 1) * BLOCK, at] = prod[BLOCK:]

    def use_near(src, q):
        near_from(grp_buf[src, q], src, q)

    loop(lambda q: near_from(cols[q], grp.me, q))

    def pair(owner, slot, src, t, dst, c):
        i, m, band = (small[owner * 3 + k, c, t] for k in range(3))
        factor = jnp.where(c < small[nseg * 3 + lax.div(owner, slots), lax.rem(owner, slots), t], scale(band), 0.0)
        prod = jnp.dot(
            ops[slot, i * 2 + band], src[m * 2 + band], preferred_element_type=jnp.float32
        )
        prod = (prod * factor).astype(jnp.bfloat16)
        dst[c, 0] = prod[:BLOCK]
        dst[c, 1] = prod[BLOCK:]

    def pass_on(q, part):
        rows = part_rows(part)
        piece = pltpu.make_async_remote_copy(
            src_ref=three.at[q, rows],
            dst_ref=left.at[q, rows],
            send_sem=pass_send.at[q, part],
            recv_sem=pass_recv.at[q, part],
            device_id={"seg": z * low + mates[0]},
            device_id_type=MESH,
        )
        if line.closing:
            piece.wait_send()
        else:
            piece.start()

    def passed(q):
        for part in range(PARTS):
            piece = left.at[q, part_rows(part)]
            pltpu.make_async_copy(piece, piece, pass_recv.at[q, part]).wait()

    def level_pairs(buf, src, c, others, own=True):
        t = src * low + y
        for mate in others:
            pair(z * low + mate, mate, buf, t, stage.at[mate, src], c)
        if own:
            pair(me, y, buf, t, far.at[t], c)

    def hand_over(src, others):
        for mate in others:
            piece = pltpu.make_async_remote_copy(
                src_ref=stage.at[mate, src],
                dst_ref=far.at[src * low + y],
                send_sem=far_send.at[mate, src],
                recv_sem=far_recv.at[src * low + y],
                device_id={"seg": z * low + mate},
                device_id_type=MESH,
            )
            if line.closing:
                piece.wait_send()
            else:
                piece.start()

    def end_copy(other):
        return pltpu.make_async_remote_copy(
            src_ref=end_stage.at[other],
            dst_ref=far.at[z * low + other],
            send_sem=end_send.at[other],
            recv_sem=far_recv.at[z * low + other],
            device_id={"seg": end * low + y},
            device_id_type=MESH,
        )

    def for_end():
        for at, buf in ((1, left), (LEVELS - 2, right)):

            @pl.when(z == at)
            def _():
                loop(lambda q: operands(low, q, buf[q]))

        @pl.when(inner)
        def _():
            for other in [y] + mates:
                t = z * low + other
                loop(
                    lambda c: pair(end * low + y, low, side.at[other], t, end_stage.at[other], c),
                    slots,
                )
                end_copy(other).start()

    def rows_copy(q):
        return pltpu.make_async_remote_copy(
            src_ref=side.at[mates[0], q],
            dst_ref=three.at[q],
            send_sem=rows_send.at[q],
            recv_sem=rows_recv.at[q],
            device_id={"seg": beside * low + y},
            device_id_type=MESH,
        )

    def turn_copy(k):
        t = (LEVELS - 1 - end) * low + y
        return pltpu.make_async_remote_copy(
            src_ref=turn_stage.at[k],
            dst_ref=far.at[t],
            send_sem=turn_send.at[k],
            recv_sem=far_recv.at[t],
            device_id={"seg": end * low + (mates[0] if k else y)},
            device_id_type=MESH,
        )

    def turn_pairs():
        t = (LEVELS - 1 - end) * low + y
        for k, owner in enumerate((y, mates[0])):
            loop(
                lambda c: pair(end * low + owner, low + k, two, t, turn_stage.at[k], c), slots
            )

    def take_turn(step):
        pl.semaphore_signal(
            go, inc=1, device_id={"grp": grp.me + step}, device_id_type=MESH
        )

    def first(q):
        line.arrive(1, q)
        grp.step(1, q, None if grp.closing else use_near)
        if not line.closing:
            for mate in mates:
                pltpu.make_async_copy(
                    side.at[mate, q], side.at[mate, q], side_recv.at[mate, q]
                ).wait()
                operands(mate, q, side[mate, q])
        if line.turns:

            @pl.when(is_end & early)
            def _():
                if line.closing:
                    rows_copy(q).wait_send()
                else:
                    rows_copy(q).start()

    def second(q):
        if line.turns and not line.closing:

            @pl.when(inner & early & (q == PIECES - 3))
            def _():
                line.closing = True
                loop(line.cross, PIECES - 3)
                line.closing = False
                take_turn(1)

        line.arrive(2, q)
        if line.turns and not line.closing:

            @pl.when(inner & late & (q == PIECES - 1))
            def _():
                take_turn(-1)

        grp.step(2, q, None if grp.closing else use_near)
        if line.turns and not line.closing:

            @pl.when(inner & early)
            def _():
                pltpu.make_async_copy(three.at[q], three.at[q], rows_recv.at[q]).wait()
                operands(low + 1, q, three[q])

        if not line.closing:

            @pl.when(q < slots)
            def _():
                for mate in mates:
                    t = z * low + mate
                    pair(me, y, side.at[mate], t, far.at[t], q)
                for here, src, _, way in line.there(1):

                    @pl.when(here)
                    def _():
                        level_pairs(line.buf(1, way), src, q, mates)

                        @pl.when(q == slots - 1)
                        def _():
                            hand_over(src, mates)

    def later(d):
        def step(q):
            if d < LEVELS:
                line.arrive(d, q, pass_on if d == LEVELS - 1 else None)
            grp.step(d, q, None if grp.closing else use_near)

        loop(step)

    def after(d):
        last = d == LEVELS - 1
        others = mates[1:] if last else mates
        for here, src, _, way in line.there(d):

            @pl.when(here)
            def _():
                if not line.closing:
                    if others:
                        loop(lambda c: level_pairs(line.buf(d, way), src, c, others, False), slots)
                hand_over(src, others)
                if not line.closing:
                    loop(lambda c: level_pairs(line.buf(d, way), src, c, ()), slots)
                if last and not line.closing:
                    loop(passed)
                    t = src * low + before
                    loop(lambda c: pair(me, y, left, t, far.at[t], c), slots)

    def landed(t, last):
        tz, ty = lax.div(t, low), lax.rem(t, low)
        across = is_end & (tz == LEVELS - 1 - z)
        passed_on = across & (ty == before)
        handed = is_end & (tz == beside) & (ty == y)
        if line.turns:
            passed_on, handed = passed_on & late, handed | (across & (ty == y) & early)
        now = across if last else jnp.logical_not(across)

        @pl.when(now & (handed | ((ty != y) & (tz != z) & jnp.logical_not(passed_on))))
        def _():
            pltpu.make_async_copy(far.at[t], far.at[t], far_recv.at[t]).wait()

    loop(first)
    own.wait()
    far[me] = jnp.zeros(far.shape[1:], far.dtype)
    for_end()
    if line.turns:

        @pl.when(inner & late)
        def _():
            pl.semaphore_wait(go, 1)
            loop(line.cross)

    loop(second)
    if line.turns:

        @pl.when(inner & early)
        def _():
            line.closing = True
            line.cross(PIECES - 3)
            line.cross(PIECES - 2)
            line.cross(PIECES - 1)
            line.closing = False
            turn_pairs()

    after(2)
    if line.turns:

        @pl.when(inner & early)
        def _():
            pl.semaphore_wait(go, 1)
            turn_copy(1).start()
            turn_copy(0).start()

    line.closing = grp.closing = True
    loop(begin)
    loop(first)
    after(1)
    loop(second)
    after(2)
    loop(lambda t: landed(t, False), nseg)
    line.closing = grp.closing = False
    for d in range(3, max(LEVELS, grp.high + 1)):
        later(d)
        if d < LEVELS:
            after(d)

    line.closing = grp.closing = True
    for d in range(3, max(LEVELS, grp.high + 1)):
        later(d)
        if d < LEVELS:
            after(d)

    @pl.when(inner)
    def _():
        for other in [y] + mates:
            end_copy(other).wait_send()

    if line.turns:

        @pl.when(inner & late)
        def _():
            loop(line.cross)

        @pl.when(inner & early)
        def _():
            for k in range(2):
                turn_copy(k).wait_send()

    loop(lambda k: landed((LEVELS - 1 - z) * low + k, True), low)


def write_kernel(near, far, near_out, far_out, near_sem, far_sem):
    copies = []
    half = far.shape[0] // 2
    for a in range(2):
        for b in range(2):
            copies.append((near.at[a, b], near_out.at[a, b], near_sem.at[a, b]))
        at = pl.ds(a * half, half)
        copies.append((far.at[at], far_out.at[at], far_sem.at[a]))
    copies = [pltpu.make_async_copy(*copy) for copy in copies]
    for copy in copies:
        copy.start()
    for copy in copies:
        copy.wait()


def body(nseg, ngrp, spectra, band_bins, far_list, far_count):
    slots = far_list.shape[3]
    low = nseg // LEVELS
    smem = pl.BlockSpec(memory_space=pltpu.SMEM)
    whole = pl.BlockSpec(memory_space=pltpu.VMEM)
    sems = pltpu.SemaphoreType.DMA
    half = jnp.bfloat16
    lists = jnp.transpose(far_list[0], (0, 3, 2, 1)).reshape(-1, slots, nseg)
    counts = far_count.reshape(-1, slots, nseg)
    bins = jnp.pad(band_bins[None], [(0, 0), (0, slots - 2), (0, nseg - 2)])
    small = jnp.concatenate([lists, counts, bins])
    near = jax.ShapeDtypeStruct((2, 2, BLK_DEV * BLOCK, ngrp * BLK_DEV * BLOCK), half)
    far = jax.ShapeDtypeStruct((nseg, slots, 2, BLOCK, BLOCK), half)
    buffers = [
        pltpu.VMEM((PIECES, DEPTH, BLOCK), half),
        pltpu.VMEM((PIECES, DEPTH, BLOCK), half),
        pltpu.VMEM((PIECES, DEPTH, BLOCK), half),
        pltpu.VMEM((PIECES, DEPTH, BLOCK), half),
        pltpu.VMEM((PIECES, DEPTH, BLOCK), half),
        pltpu.VMEM((low, PIECES, DEPTH, BLOCK), half),
        pltpu.VMEM((ngrp, PIECES, DEPTH, BLOCK), half),
        pltpu.VMEM((low + (2 if low == 2 else 1), PIECES, 2 * BLOCK, DEPTH), half),
        pltpu.VMEM((low, LEVELS, slots, 2, BLOCK, BLOCK), half),
        pltpu.VMEM((low, slots, 2, BLOCK, BLOCK), half),
    ]
    kept = sum(math.prod(a.shape) * 2 for a in buffers + [near, far, spectra])
    vmem = min(kept + 2 * 1024**2, LIMIT)
    near_shape, far_shape = near, far
    near, far = pl.pallas_call(
        functools.partial(kernel, nseg, ngrp),
        out_shape=(near, far),
        in_specs=[smem, whole],
        out_specs=(whole, whole),
        scratch_shapes=buffers
        + [

            sems((2, LEVELS, PIECES, PARTS)),
            sems((LEVELS, PIECES, PARTS)),
            sems((low, PIECES)),
            sems((low, PIECES)),
            sems((4, ngrp, PIECES)),
            sems((ngrp, PIECES)),
            sems((low, LEVELS)),
            sems((low,)),
            sems((nseg,)),
            sems((PIECES, PARTS)),
            sems((PIECES, PARTS)),
            pltpu.VMEM((2, slots, 2, BLOCK, BLOCK), half),
            sems((2,)),
            sems((PIECES,)),
            sems((PIECES,)),
            pltpu.SemaphoreType.REGULAR,
            sems,
        ],
        compiler_params=pltpu.CompilerParams(
            collective_id=0, has_side_effects=True, vmem_limit_bytes=vmem
        ),
    )(small, spectra)
    near, far = pl.pallas_call(
        write_kernel,
        out_shape=(near_shape, far_shape),
        in_specs=[pl.BlockSpec(memory_space=pl.ANY)] * 2,
        out_specs=[pl.BlockSpec(memory_space=pl.ANY)] * 2,
        scratch_shapes=[sems((2, 2)), sems((2,))],
        compiler_params=pltpu.CompilerParams(vmem_limit_bytes=1024**2),
    )(near, far)
    return (near, far[None, None])


def solution(mesh):
    placed = (
        P(None, None, None, ("seg", "grp")),
        P(),
        P("grp", None, None, None, None),
        P("grp", None, None),
    )
    return jax.shard_map(
        functools.partial(body, mesh.shape["seg"], mesh.shape["grp"]),
        mesh=mesh,
        in_specs=placed,
        out_specs=(
            P(None, None, ("seg", "grp"), None),
            P("seg", "grp", None, None, None, None, None),
        ),
        check_vma=False,
    )
```

```python
import functools
import math

import jax
import jax.numpy as jnp
from jax import lax
from jax.experimental import pallas as pl
from jax.experimental.pallas import tpu as pltpu
from jax.sharding import PartitionSpec as P

W = 8
F = 128
BAND_MAX = 48
SMOOTH = 4
BLOCK = 128
BLK_DEV = 3
DEPTH = W * 2 * BAND_MAX
PIECES = 2 * BLK_DEV
LEVELS = 4
PARTS = 2
LIMIT = 62 * 1024**2
CORES = 2


HIGH = lax.Precision.HIGHEST
MESH = pl.DeviceIdType.MESH


def whiten(m, small, spec, cols):
    power = jnp.zeros((F, BLOCK), jnp.float32)
    for w in range(W):
        for p in range(2):
            values = spec[w, p, :, m * BLOCK : (m + 1) * BLOCK].astype(jnp.float32)
            power = power + values * values
    f = lax.broadcasted_iota(jnp.int32, (F, F), 0)
    g = lax.broadcasted_iota(jnp.int32, (F, F), 1)
    window = jnp.where(jnp.abs(f - g) <= SMOOTH, 1.0, 0.0).astype(jnp.float32)
    totals = jnp.sum(window, axis=1, keepdims=True) * W
    level = jnp.dot(window, power, precision=HIGH, preferred_element_type=jnp.float32) / totals
    gain = lax.rsqrt(level + 1e-06)
    here = slice(m * BLOCK, (m + 1) * BLOCK)
    ahead = jnp.full((BAND_MAX, BLOCK), small[small.shape[0] - 1, 0, 0], jnp.int32) == 0
    for p in range(2):
        for w in range(W):
            at = slice((p * W + w) * BAND_MAX, (p * W + w + 1) * BAND_MAX)
            low = spec[w, p, :BAND_MAX, here].astype(jnp.float32) * gain[:BAND_MAX]
            high = spec[w, p, F - BAND_MAX :, here].astype(jnp.float32) * gain[F - BAND_MAX :]
            cols[m * 2, at] = jnp.where(ahead, low, high).astype(jnp.bfloat16)
            cols[m * 2 + 1, at] = jnp.where(ahead, high, low).astype(jnp.bfloat16)


class Gather:
    def __init__(self, axis, high, low, own, buf, send, recv):
        self.axis, self.high, self.low = axis, high, low
        self.own, self.buf, self.send, self.recv = own, buf, send, recv
        self.me = lax.axis_index(axis)
        self.p, self.l = lax.div(self.me, low), lax.rem(self.me, low)
        p, l = self.p, self.l
        self.dirs = [
            (p + 1 < high, self.me + low),
            (p > 0, self.me - low),
            (l + 1 < low, self.me + 1),
            (l > 0, self.me - 1),
        ]
        if high == 1:
            self.dirs[0] = self.dirs[1] = None
        if low == 1:
            self.dirs[2] = self.dirs[3] = None
        self.closing = False

    def greet(self, barrier):
        for entry in self.dirs:
            if entry is not None:

                @pl.when(entry[0])
                def _():
                    pl.semaphore_signal(
                        barrier, inc=1, device_id={self.axis: entry[1]}, device_id_type=MESH
                    )

    def peers(self):
        return sum(jnp.where(entry[0], 1, 0) for entry in self.dirs if entry is not None)

    def copy(self, way, src, q, own):
        return pltpu.make_async_remote_copy(
            src_ref=self.own.at[q] if own else self.buf.at[src, q],
            dst_ref=self.buf.at[src, q],
            send_sem=self.send.at[way, src, q],
            recv_sem=self.recv.at[src, q],
            device_id={self.axis: self.dirs[way][1]},
            device_id_type=MESH,
        )

    def pass_on(self, ways, src, q, own=False):
        for way in ways:
            if self.dirs[way] is not None:

                @pl.when(self.dirs[way][0])
                def _():
                    piece = self.copy(way, src, q, own)
                    if self.closing:
                        piece.wait_send()
                    else:
                        piece.start()

    def arrive(self, there, src, q, ways, use):
        @pl.when(there)
        def _():
            if not self.closing:
                pltpu.make_async_copy(
                    self.buf.at[src, q], self.buf.at[src, q], self.recv.at[src, q]
                ).wait()
            self.pass_on(ways, src, q)
            if use is not None and not self.closing:
                use(src, q)

    def start(self, q):
        self.pass_on((0, 1, 2, 3), self.me, q, own=True)

    def step(self, st, q, use, low_first=False):
        p, l, low = self.p, self.l, self.low
        turn = () if low_first else (2, 3)
        if 0 < st < self.high:
            self.arrive(p - st >= 0, (p - st) * low + l, q, (0,) + turn, use)
            self.arrive(p + st < self.high, (p + st) * low + l, q, (1,) + turn, use)
        d = st - 1
        if not 0 <= d < self.high:
            return
        for far, way in [(p, None)] if d == 0 else [(p - d, 0), (p + d, 1)]:
            inside = (far >= 0) & (far < self.high)
            for e in range(1, low):
                for there, other, on in ((l - e >= 0, l - e, 2), (l + e < low, l + e, 3)):
                    if not low_first:
                        ways = (on,)
                    elif d == 0:
                        ways = (0, 1, on)
                    else:
                        ways = (way,)
                    self.arrive(inside & there, far * low + other, q, ways, use)


def part_rows(part):
    return pl.ds(part * (DEPTH // PARTS), DEPTH // PARTS)


class Line:
    def __init__(self, low, own, bufs, send, recv):
        self.low, self.own, self.bufs, self.send, self.recv = low, own, bufs, send, recv
        self.me = lax.axis_index("seg")
        self.z = lax.div(self.me, low)
        self.late = lax.rem(lax.axis_index("grp"), CORES) == CORES - 1
        self.turns = low == 2 and CORES == 2
        self.closing = False

    def slot(self, d, way):
        return d if d > 1 else 1 - way

    def buf(self, d, way):
        return self.bufs[self.slot(d, way)]

    def move(self, way, d, q, part):
        at = self.slot(d + 1, way)
        rows = part_rows(part)
        piece = pltpu.make_async_remote_copy(
            src_ref=(self.buf(d, way) if d else self.own).at[q, rows],
            dst_ref=self.bufs[at].at[q, rows],
            send_sem=self.send.at[way, d, q, part],
            recv_sem=self.recv.at[at, q, part],
            device_id={"seg": self.me + (self.low if way else -self.low)},
            device_id_type=MESH,
        )
        if self.closing:
            piece.wait_send()
        else:
            piece.start()

    def start(self, q):
        z = self.z

        @pl.when((z + 1 < LEVELS) & (z != LEVELS - 2))
        def _():
            for part in range(PARTS):
                self.move(1, 0, q, part)

        @pl.when((z > 0) & (z != 1))
        def _():
            for part in range(PARTS):
                self.move(0, 0, q, part)

    def there(self, d):
        z = self.z
        left, right = z - d >= 0, z + d < LEVELS
        on_right, on_left = z + 1 < LEVELS, z > 0
        if d == 1:
            left, right = left & (z != LEVELS - 1), right & (z != 0)
        if self.turns and d == 1:
            first = jnp.logical_not(self.late) & (not self.closing)
            on_right, on_left = on_right & (first | (z != 1)), on_left & (first | (z != LEVELS - 2))
        elif self.turns and d == 2:
            on_right, on_left = on_right & self.late, on_left & self.late
        elif self.turns:
            left, right = left & self.late, right & self.late
        return ((left, z - d, on_right, 1), (right, z + d, on_left, 0))

    def cross(self, q):
        for at, way in ((1, 1), (LEVELS - 2, 0)):

            @pl.when(self.z == at)
            def _():
                for part in range(PARTS):
                    self.move(way, 1, q, part)

    def arrive(self, d, q, then=None):
        for part in range(PARTS):
            for here, _, on, way in self.there(d):

                @pl.when(here)
                def _():
                    if not self.closing:
                        at = self.slot(d, way)
                        piece = self.bufs[at].at[q, part_rows(part)]
                        pltpu.make_async_copy(piece, piece, self.recv.at[at, q, part]).wait()

                    if d + 1 < LEVELS:

                        @pl.when(on)
                        def _():
                            self.move(way, d, q, part)

                    if then is not None:
                        then(q, part)


def kernel(
    nseg, ngrp, small, spec, near, far, cols, left, right, two, three, side, grp_buf, ops, stage, end_stage,
    line_send, line_recv, side_send, side_recv, grp_send, grp_recv,
    far_send, end_send, far_recv, pass_send, pass_recv,
    turn_stage, turn_send, rows_send, rows_recv, go, move,
    turn_in, over_send, over_recv,
):
    low = nseg // LEVELS
    slots = far.shape[1]
    line = Line(low, cols, (left, right, two, three), line_send, line_recv)
    grp = Gather("grp", ngrp // CORES, CORES, cols, grp_buf, grp_send, grp_recv)
    me, z = line.me, line.z
    y = lax.rem(me, low)
    mates = [lax.rem(y + e, low) for e in range(1, low)]
    before = lax.rem(y + low - 1, low)
    is_end = (z == 0) | (z == LEVELS - 1)
    inner = (z == 1) | (z == LEVELS - 2)
    end = jnp.where(z == 1, 0, LEVELS - 1)
    beside = jnp.where(z == 0, 1, LEVELS - 2)

    barrier = pltpu.get_barrier_semaphore()

    def greet(seg):
        pl.semaphore_signal(barrier, inc=1, device_id={"seg": seg}, device_id_type=MESH)

    for on, seg in ((z + 1 < LEVELS, me + low), (z > 0, me - low)):

        @pl.when(on)
        def _():
            greet(seg)

    for mate in mates:
        greet(z * low + mate)
        if line.turns:

            @pl.when(is_end)
            def _():
                greet(beside * low + mate)

    late = line.late
    early = jnp.logical_not(late)
    grp.greet(barrier)

    def side_copy(e, q):
        return pltpu.make_async_remote_copy(
            src_ref=cols.at[q],
            dst_ref=side.at[y, q],
            send_sem=side_send.at[e, q],
            recv_sem=side_recv.at[y, q],
            device_id={"seg": z * low + mates[e]},
            device_id_type=MESH,
        )

    def begin(q):
        line.start(q)
        for e in range(low - 1):
            if line.closing:
                side_copy(e, q).wait_send()
            else:
                side_copy(e, q).start()
        grp.start(q)

    def loop(fn, count=PIECES):
        def step(q, carry):
            fn(q)
            return carry

        lax.fori_loop(0, count, step, 0)

    for m in range(BLK_DEV):
        whiten(m, small, spec, cols)
        if m == 0:
            inner_peers = jnp.where(z + 1 < LEVELS, 1, 0) + jnp.where(z > 0, 1, 0)
            if line.turns:
                inner_peers += jnp.where(inner, low - 1, 0)
            pl.semaphore_wait(barrier, inner_peers + (low - 1) + grp.peers())
        begin(2 * m)
        begin(2 * m + 1)

    own = pltpu.make_async_copy(cols, side.at[y], move)
    own.start()

    half = DEPTH // 2

    def operands(slot, q, piece):
        band = lax.rem(q, 2)
        bin_of = lax.rem(lax.broadcasted_iota(jnp.int32, (1, DEPTH), 1), BAND_MAX)
        live = jnp.where(bin_of < small[small.shape[0] - 1, band, 1], 1.0, 0.0).astype(jnp.float32)
        rows = jnp.transpose(piece.astype(jnp.float32)) * live
        ops[slot, q, :BLOCK] = rows.astype(jnp.bfloat16)
        ops[slot, q, BLOCK:, :half] = rows[:, half:].astype(jnp.bfloat16)
        ops[slot, q, BLOCK:, half:] = (-rows[:, :half]).astype(jnp.bfloat16)

    line.arrive(1, 0)
    loop(lambda q: operands(y, q, cols[q]))

    def scale(band):
        return lax.rsqrt(jnp.full((1, BLOCK), W * small[small.shape[0] - 1, band, 1], jnp.int32).astype(jnp.float32))

    def near_from(piece, src, q):
        m, band = lax.div(q, 2), lax.rem(q, 2)
        at = pl.ds(pl.multiple_of(src * (BLK_DEV * BLOCK) + m * BLOCK, BLOCK), BLOCK)
        for i in range(BLK_DEV):
            prod = jnp.dot(ops[y, i * 2 + band], piece, preferred_element_type=jnp.float32)
            prod = (prod * scale(band)).astype(jnp.bfloat16)
            near[band, 0, i * BLOCK : (i + 1) * BLOCK, at] = prod[:BLOCK]
            near[band, 1, i * BLOCK : (i + 1) * BLOCK, at] = prod[BLOCK:]

    def use_near(src, q):
        near_from(grp_buf[src, q], src, q)

    def pair(owner, slot, src, t, dst, c):
        i, m, band = (small[owner * 3 + k, c, t] for k in range(3))
        factor = jnp.where(c < small[nseg * 3 + lax.div(owner, slots), lax.rem(owner, slots), t], scale(band), 0.0)
        prod = jnp.dot(
            ops[slot, i * 2 + band], src[m * 2 + band], preferred_element_type=jnp.float32
        )
        prod = (prod * factor).astype(jnp.bfloat16)
        dst[c, 0] = prod[:BLOCK]
        dst[c, 1] = prod[BLOCK:]

    def pass_on(q, part):
        rows = part_rows(part)
        piece = pltpu.make_async_remote_copy(
            src_ref=three.at[q, rows],
            dst_ref=left.at[q, rows],
            send_sem=pass_send.at[q, part],
            recv_sem=pass_recv.at[q, part],
            device_id={"seg": z * low + mates[0]},
            device_id_type=MESH,
        )
        if line.closing:
            piece.wait_send()
        else:
            piece.start()

    def passed(q):
        for part in range(PARTS):
            piece = left.at[q, part_rows(part)]
            pltpu.make_async_copy(piece, piece, pass_recv.at[q, part]).wait()

    def level_pairs(buf, src, c, others, own=True):
        t = src * low + y
        for mate in others:
            pair(z * low + mate, mate, buf, t, stage.at[mate, src], c)
        if own:
            pair(me, y, buf, t, far.at[t], c)

    def hand_over(src, others):
        for mate in others:
            piece = pltpu.make_async_remote_copy(
                src_ref=stage.at[mate, src],
                dst_ref=far.at[src * low + y],
                send_sem=far_send.at[mate, src],
                recv_sem=far_recv.at[src * low + y],
                device_id={"seg": z * low + mate},
                device_id_type=MESH,
            )
            if line.closing:
                piece.wait_send()
            else:
                piece.start()

    def end_copy(other):
        return pltpu.make_async_remote_copy(
            src_ref=end_stage.at[other],
            dst_ref=far.at[z * low + other],
            send_sem=end_send.at[other],
            recv_sem=far_recv.at[z * low + other],
            device_id={"seg": end * low + y},
            device_id_type=MESH,
        )

    def for_end():
        for at, buf in ((1, left), (LEVELS - 2, right)):

            @pl.when(z == at)
            def _():
                loop(lambda q: operands(low, q, buf[q]))

        @pl.when(inner)
        def _():
            for other in [y] + mates:
                t = z * low + other
                loop(
                    lambda c: pair(end * low + y, low, side.at[other], t, end_stage.at[other], c),
                    slots,
                )
                end_copy(other).start()

    def rows_copy(q):
        return pltpu.make_async_remote_copy(
            src_ref=side.at[mates[0], q],
            dst_ref=three.at[q],
            send_sem=rows_send.at[q],
            recv_sem=rows_recv.at[q],
            device_id={"seg": beside * low + y},
            device_id_type=MESH,
        )

    def turn_copy(k):
        t = (LEVELS - 1 - end) * low + (before if k else y)
        return pltpu.make_async_remote_copy(
            src_ref=turn_in if k else turn_stage.at[0],
            dst_ref=far.at[t],
            send_sem=turn_send.at[k],
            recv_sem=far_recv.at[t],
            device_id={"seg": end * low + y},
            device_id_type=MESH,
        )

    def turn_over():
        return pltpu.make_async_remote_copy(
            src_ref=turn_stage.at[1],
            dst_ref=turn_in,
            send_sem=over_send,
            recv_sem=over_recv,
            device_id={"seg": z * low + mates[0]},
            device_id_type=MESH,
        )

    def turn_pairs():
        t = (LEVELS - 1 - end) * low + y
        for k, owner in ((1, mates[0]), (0, y)) if line.turns else ():
            loop(
                lambda c: pair(end * low + owner, low + k, two, t, turn_stage.at[k], c), slots
            )
            if k:
                turn_over().start()

    def take_turn(step):
        pl.semaphore_signal(
            go, inc=1, device_id={"grp": grp.me + step}, device_id_type=MESH
        )

    def first(q):
        if line.closing:
            line.arrive(1, q)
        else:

            @pl.when(q > 0)
            def _():
                line.arrive(1, q)

            near_from(cols[q], grp.me, q)
        grp.step(1, q, None if grp.closing else use_near)
        if not line.closing:
            for mate in mates:
                pltpu.make_async_copy(
                    side.at[mate, q], side.at[mate, q], side_recv.at[mate, q]
                ).wait()
                operands(mate, q, side[mate, q])
        if line.turns:

            @pl.when(is_end & early)
            def _():
                if line.closing:
                    rows_copy(q).wait_send()
                else:
                    rows_copy(q).start()

    def second(q):
        if line.turns and not line.closing:

            @pl.when(inner & early & (q == PIECES - 3))
            def _():
                line.closing = True
                loop(line.cross, PIECES - 3)
                line.closing = False
                take_turn(1)

        line.arrive(2, q)
        if line.turns and not line.closing:

            @pl.when(inner & late & (q == PIECES - 1))
            def _():
                take_turn(-1)

        grp.step(2, q, None if grp.closing else use_near)
        if line.turns and not line.closing:

            @pl.when(inner & early)
            def _():
                pltpu.make_async_copy(three.at[q], three.at[q], rows_recv.at[q]).wait()
                operands(low + 1, q, three[q])

        if not line.closing:

            @pl.when(q < slots)
            def _():
                for mate in mates:
                    t = z * low + mate
                    pair(me, y, side.at[mate], t, far.at[t], q)
                for here, src, _, way in line.there(1):

                    @pl.when(here)
                    def _():
                        level_pairs(line.buf(1, way), src, q, mates)

                        @pl.when(q == slots - 1)
                        def _():
                            hand_over(src, mates)

    def later(d):
        def step(q):
            if d < LEVELS:
                line.arrive(d, q, pass_on if d == LEVELS - 1 else None)
            grp.step(d, q, None if grp.closing else use_near)

        loop(step)

    def after(d):
        last = d == LEVELS - 1
        others = mates[1:] if last else mates
        for here, src, _, way in line.there(d):

            @pl.when(here)
            def _():
                if not line.closing:
                    if others:
                        loop(lambda c: level_pairs(line.buf(d, way), src, c, others, False), slots)
                hand_over(src, others)
                if not line.closing:
                    loop(lambda c: level_pairs(line.buf(d, way), src, c, ()), slots)
                if last and not line.closing:
                    loop(passed)
                    t = src * low + before
                    loop(lambda c: pair(me, y, left, t, far.at[t], c), slots)

    def landed(t, last):
        tz, ty = lax.div(t, low), lax.rem(t, low)
        across = is_end & (tz == LEVELS - 1 - z)
        passed_on = across & (ty == before)
        handed = is_end & (tz == beside) & (ty == y)
        if line.turns:
            passed_on, handed = passed_on & late, handed | (across & (ty == y) & early)
        now = across if last else jnp.logical_not(across)

        @pl.when(now & (handed | ((ty != y) & (tz != z) & jnp.logical_not(passed_on))))
        def _():
            pltpu.make_async_copy(far.at[t], far.at[t], far_recv.at[t]).wait()

    loop(first)
    own.wait()
    far[me] = jnp.zeros(far.shape[1:], far.dtype)
    for_end()
    if line.turns:

        @pl.when(inner & late)
        def _():
            pl.semaphore_wait(go, 1)
            loop(line.cross)

    loop(second)
    if line.turns:

        @pl.when(inner & early)
        def _():
            line.closing = True
            line.cross(PIECES - 3)
            line.cross(PIECES - 2)
            line.cross(PIECES - 1)
            line.closing = False
            turn_pairs()

    after(2)
    if line.turns:

        @pl.when(inner & early)
        def _():
            pl.semaphore_wait(go, 1)
            turn_copy(0).start()
            pltpu.make_async_copy(turn_in, turn_in, over_recv).wait()
            turn_copy(1).start()

    line.closing = grp.closing = True
    loop(begin)
    loop(first)
    after(1)
    loop(second)
    after(2)
    loop(lambda t: landed(t, False), nseg)
    line.closing = grp.closing = False
    for d in range(3, max(LEVELS, grp.high + 1)):
        later(d)
        if d < LEVELS:
            after(d)

    line.closing = grp.closing = True
    for d in range(3, max(LEVELS, grp.high + 1)):
        later(d)
        if d < LEVELS:
            after(d)

    @pl.when(inner)
    def _():
        for other in [y] + mates:
            end_copy(other).wait_send()

    if line.turns:

        @pl.when(inner & late)
        def _():
            loop(line.cross)

        @pl.when(inner & early)
        def _():
            turn_over().wait_send()
            for k in range(2):
                turn_copy(k).wait_send()

    loop(lambda k: landed((LEVELS - 1 - z) * low + k, True), low)


def write_kernel(near, far, near_out, far_out, near_sem, far_sem):
    copies = []
    half = far.shape[0] // 2
    for a in range(2):
        for b in range(2):
            copies.append((near.at[a, b], near_out.at[a, b], near_sem.at[a, b]))
        at = pl.ds(a * half, half)
        copies.append((far.at[at], far_out.at[at], far_sem.at[a]))
    copies = [pltpu.make_async_copy(*copy) for copy in copies]
    for copy in copies:
        copy.start()
    for copy in copies:
        copy.wait()


def body(nseg, ngrp, spectra, band_bins, far_list, far_count):
    slots = far_list.shape[3]
    low = nseg // LEVELS
    smem = pl.BlockSpec(memory_space=pltpu.SMEM)
    whole = pl.BlockSpec(memory_space=pltpu.VMEM)
    sems = pltpu.SemaphoreType.DMA
    half = jnp.bfloat16
    lists = jnp.transpose(far_list[0], (0, 3, 2, 1)).reshape(-1, slots, nseg)
    counts = far_count.reshape(-1, slots, nseg)
    bins = jnp.pad(band_bins[None], [(0, 0), (0, slots - 2), (0, nseg - 2)])
    small = jnp.concatenate([lists, counts, bins])
    near = jax.ShapeDtypeStruct((2, 2, BLK_DEV * BLOCK, ngrp * BLK_DEV * BLOCK), half)
    far = jax.ShapeDtypeStruct((nseg, slots, 2, BLOCK, BLOCK), half)
    buffers = [
        pltpu.VMEM((PIECES, DEPTH, BLOCK), half),
        pltpu.VMEM((PIECES, DEPTH, BLOCK), half),
        pltpu.VMEM((PIECES, DEPTH, BLOCK), half),
        pltpu.VMEM((PIECES, DEPTH, BLOCK), half),
        pltpu.VMEM((PIECES, DEPTH, BLOCK), half),
        pltpu.VMEM((low, PIECES, DEPTH, BLOCK), half),
        pltpu.VMEM((ngrp, PIECES, DEPTH, BLOCK), half),
        pltpu.VMEM((low + (2 if low == 2 else 1), PIECES, 2 * BLOCK, DEPTH), half),
        pltpu.VMEM((low, LEVELS, slots, 2, BLOCK, BLOCK), half),
        pltpu.VMEM((low, slots, 2, BLOCK, BLOCK), half),
    ]
    kept = sum(math.prod(a.shape) * 2 for a in buffers + [near, far, spectra])
    vmem = min(kept + 2 * 1024**2, LIMIT)
    near_shape, far_shape = near, far
    near, far = pl.pallas_call(
        functools.partial(kernel, nseg, ngrp),
        out_shape=(near, far),
        in_specs=[smem, whole],
        out_specs=(whole, whole),
        scratch_shapes=buffers
        + [

            sems((2, LEVELS, PIECES, PARTS)),
            sems((LEVELS, PIECES, PARTS)),
            sems((low, PIECES)),
            sems((low, PIECES)),
            sems((4, ngrp, PIECES)),
            sems((ngrp, PIECES)),
            sems((low, LEVELS)),
            sems((low,)),
            sems((nseg,)),
            sems((PIECES, PARTS)),
            sems((PIECES, PARTS)),
            pltpu.VMEM((2, slots, 2, BLOCK, BLOCK), half),
            sems((2,)),
            sems((PIECES,)),
            sems((PIECES,)),
            pltpu.SemaphoreType.REGULAR,
            sems,
            pltpu.VMEM((slots, 2, BLOCK, BLOCK), half),
            sems,
            sems,
        ],
        compiler_params=pltpu.CompilerParams(
            collective_id=0, has_side_effects=True, vmem_limit_bytes=vmem
        ),
    )(small, spectra)
    near, far = pl.pallas_call(
        write_kernel,
        out_shape=(near_shape, far_shape),
        in_specs=[pl.BlockSpec(memory_space=pl.ANY)] * 2,
        out_specs=[pl.BlockSpec(memory_space=pl.ANY)] * 2,
        scratch_shapes=[sems((2, 2)), sems((2,))],
        compiler_params=pltpu.CompilerParams(vmem_limit_bytes=1024**2),
    )(near, far)
    return (near, far[None, None])


def solution(mesh):
    placed = (
        P(None, None, None, ("seg", "grp")),
        P(),
        P("grp", None, None, None, None),
        P("grp", None, None),
    )
    return jax.shard_map(
        functools.partial(body, mesh.shape["seg"], mesh.shape["grp"]),
        mesh=mesh,
        in_specs=placed,
        out_specs=(
            P(None, None, ("seg", "grp"), None),
            P("seg", "grp", None, None, None, None, None),
        ),
        check_vma=False,
    )
```
